512 devices in a mesh: dom: 128 (over z, y, x_hi), rel: 4 (over x_lo, core).
Axes of the slice: x: 4 (x_hi: 2, x_lo: 2; x = x_hi * 2 + x_lo), y: 4, z: 16, core: 2. Of those that a mesh axis runs over, the one named last changes fastest.
Arguments:
- entities: float32 [131072, 400], P(('dom', 'rel')), may hold values from -1.5 to 1.5
- entity_state: float32 [131072], P(('dom', 'rel')), may hold values from 0.005 to 0.1
- relations: float32 [2560, 400], replicated, may hold values from -6 to 6
- relation_state: float32 [2560], replicated, may hold values from 0.01 to 0.3
- src_rows: int32 [128, 2, 1024], P('dom', None, 'rel'), may hold values from 0 to 1023
- rel_ids: int32 [128, 2, 1024], P('dom', None, 'rel'), may hold values from 0 to 2559
- dst_rows: int32 [128, 2, 1024], P('dom', None, 'rel'), may hold values from 0 to 1023
- live_count: int32 [128, 2, 4], P('dom', None, 'rel'), may hold values from 1 to 256, as said below
- neg_rows: int32 [128, 2, 1024], P('dom'), may hold values from 0 to 1023
Outputs:
- new_entities: float32 [131072, 400], P(('dom', 'rel'))
- new_entity_state: float32 [131072], P(('dom', 'rel'))
- new_relations: float32 [2560, 400], replicated
- new_relation_state: float32 [2560], replicated
The draws below stay inside these ranges and needn't reach their ends.
Inputs may be any that keep to these rules, and one draw needn't show every extreme that they name: `live_count`: in each bucket and round exactly one of the 4 slots holds more than 128 live edges and the others at most 64; in every round some bucket has a full slot.
All inputs are finite; a program needn't handle non-finite values.
Results may differ from the reference program's by a relative error of at most 0.0003.
Values sent between devices are 32-bit elements; how exact they have to be, the bound alone decides.
No kernel may reach another device: no remote copies, remote signals or barrier semaphores. Data moves between devices by JAX's collectives and lax.ppermute only.
A program may use at most 128 MiB of HBM per device.

```python
import math
import jax
import jax.numpy as jnp
import numpy as np
from jax import lax

D = 400
RELATIONS = 2560
NEG = 1024
ROUNDS = 2
ROWS = 1024
CAP = 256
ENTITIES = 131072
N_DOM = 128
N_REL = 4


def draw_live_count(key, part):
    key = jax.random.fold_in(key, 11)
    keys = jax.random.split(key, 4)
    light = jax.random.randint(keys[0], (N_DOM, ROUNDS, N_REL), 1, CAP // 4 + 1)
    heavy = jax.random.randint(keys[1], (N_DOM, ROUNDS), CAP // 2 + 1, CAP + 1)
    chosen = jax.random.randint(keys[2], (N_DOM, ROUNDS), 0, N_REL)
    fullest = jax.random.randint(keys[3], (ROUNDS,), 0, N_DOM)
    heavy = jnp.where(jnp.arange(N_DOM)[:, None] == fullest[None, :], CAP, heavy)
    picked = jnp.arange(N_REL)[None, None, :] == chosen[:, :, None]
    return jnp.where(picked, heavy[:, :, None], light).astype(jnp.int32)


def touch_ends(values, key, least, high):
    index_at = [jax.random.randint(jax.random.fold_in(key, axis), (), 0, length) for axis, length in enumerate(values.shape)]
    longest = values.shape.index(max(values.shape))
    next_to = index_at[:longest] + [(index_at[longest] + 1) % values.shape[longest]] + index_at[longest + 1:]
    return values.at[tuple(index_at)].set(least).at[tuple(next_to)].set(high)


def level_of(own_key, dims, shards, low, largest):
    level, own = 1.0, jax.random.fold_in(own_key, 6)
    for axis_at, blocks in shards:
        draws = jnp.exp(jax.random.uniform(jax.random.fold_in(own, axis_at), (blocks,), jnp.float32, low / len(shards), largest / len(shards)))
        level = level * jnp.repeat(draws, dims[axis_at] // blocks).reshape([-1 if axis == axis_at else 1 for axis in range(len(dims))])
    return level


def cumulative_ranks(number_of, slope):
    loads = [(1 << 20) // math.isqrt(rank ** slope) + 1 for rank in range(1, number_of + 1)]
    scale = 1 + sum(loads) // (1 << 30)
    return np.cumsum(np.array([max(1, weight // scale) for weight in loads]))


def ranked_ids(own_key, extent, number_of, slope):
    listing = cumulative_ranks(number_of, slope)
    lot = jax.random.randint(jax.random.fold_in(own_key, 1), extent, 0, int(listing[number_of - 1]))
    grade = jnp.searchsorted(jnp.asarray(listing, jnp.int32), lot, side="right")
    return jax.random.permutation(jax.random.fold_in(own_key, 2), number_of)[grade].astype(jnp.int32)


def normal_values(own_key, dims, deviation, most, shards=(), held_as=jnp.bfloat16):
    level = level_of(own_key, dims, shards, -0.22, 0.18) if shards else 1.0
    values = jax.random.normal(own_key, dims, jnp.float32) * deviation * level
    return jnp.minimum(jnp.maximum(values, -most), most).astype(held_as)


def setup_inputs(seed: int = 0) -> dict:
    arg_keys = jax.random.split(jax.random.key(seed), 10)
    return {
        "entities": normal_values(arg_keys[0], (ENTITIES, D), 0.25, 1.5, ((0, 512),), jnp.float32),
        "entity_state": jnp.clip(jnp.exp(math.log(0.1) - 2.9957323 * jax.random.uniform(arg_keys[1], (ENTITIES,), jnp.float32) ** level_of(arg_keys[1], (ENTITIES,), ((0, 512),), -0.2, 0.2)), 0.005, 0.1),
        "relations": normal_values(arg_keys[2], (RELATIONS, D), 1.0, 6.0, (), jnp.float32),
        "relation_state": jnp.clip(jnp.exp(jax.random.uniform(arg_keys[3], (RELATIONS,), jnp.float32, math.log(0.01), math.log(0.3))), 0.01, 0.3),
        "src_rows": touch_ends(jax.random.randint(arg_keys[4], (N_DOM, ROUNDS, N_REL * CAP), 0, ROWS), jax.random.fold_in(arg_keys[4], 1), 0, ROWS - 1).astype(jnp.int32),
        "rel_ids": touch_ends(ranked_ids(arg_keys[5], (N_DOM, ROUNDS, N_REL * CAP), RELATIONS, 1), jax.random.fold_in(arg_keys[5], 3), 0, RELATIONS - 1).astype(jnp.int32),
        "dst_rows": touch_ends(jax.random.randint(arg_keys[6], (N_DOM, ROUNDS, N_REL * CAP), 0, ROWS), jax.random.fold_in(arg_keys[6], 1), 0, ROWS - 1).astype(jnp.int32),
        "live_count": draw_live_count(jax.random.fold_in(arg_keys[9], 71), 0),
        "neg_rows": touch_ends(jax.random.randint(arg_keys[8], (N_DOM, ROUNDS, NEG), 0, ROWS), jax.random.fold_in(arg_keys[8], 1), 0, ROWS - 1).astype(jnp.int32),
    }


HIGHEST = lax.Precision.HIGHEST
LEARN_RATE = 0.1
EPSILON = 1e-08

def complex_product(first, second):
    half = first.shape[-1] // 2
    real_part = first[:, :half] * second[:, :half] - first[:, half:] * second[:, half:]
    imag_part = first[:, :half] * second[:, half:] + first[:, half:] * second[:, :half]
    return jnp.concatenate([real_part, imag_part], axis=1)

def complex_back(upstream, first, second):
    half = first.shape[-1] // 2
    up_real, up_imag = (upstream[:, :half], upstream[:, half:])
    d_first = jnp.concatenate([up_real * second[:, :half] + up_imag * second[:, half:], up_imag * second[:, :half] - up_real * second[:, half:]], axis=1)
    d_second = jnp.concatenate([up_real * first[:, :half] + up_imag * first[:, half:], up_imag * first[:, :half] - up_real * first[:, half:]], axis=1)
    return (d_first, d_second)

def edge_terms(source_slab, target_slab, table, source_list, kind_list, target_list, live_mask, negatives):
    head_vec = source_slab[source_list]
    rel_vec = table[kind_list]
    tail_vec = target_slab[target_list]
    neg_table = target_slab[negatives]
    product = complex_product(head_vec, rel_vec)
    pos_score = lax.optimization_barrier(jnp.sum(product * tail_vec, axis=1))
    scores = jnp.dot(product, neg_table.T, precision=HIGHEST, preferred_element_type=jnp.float32)
    pos_weight = -jax.nn.sigmoid(-pos_score) * live_mask
    neg_weight = jax.nn.sigmoid(scores) * (live_mask / NEG)[:, None]
    d_product = pos_weight[:, None] * tail_vec + jnp.dot(neg_weight, neg_table, precision=HIGHEST, preferred_element_type=jnp.float32)
    d_negset = jnp.dot(neg_weight.T, product, precision=HIGHEST, preferred_element_type=jnp.float32)
    d_head, d_rel = complex_back(d_product, head_vec, rel_vec)
    grad_source = jnp.zeros_like(source_slab).at[source_list].add(d_head)
    grad_target = jnp.zeros_like(target_slab).at[target_list].add(pos_weight[:, None] * product)
    grad_target = grad_target.at[negatives].add(d_negset)
    return (grad_source, grad_target, d_rel)

def reference(entities, entity_state, relations, relation_state, src_rows, rel_ids, dst_rows, live_count, neg_rows):
    slabs = entities.reshape(N_DOM, ROWS, D)
    states = entity_state.reshape(N_DOM, ROWS)
    positions = (jnp.arange(N_REL * CAP) % CAP).astype(jnp.int32)
    slot_of = (jnp.arange(N_REL * CAP) // CAP).astype(jnp.int32)
    rel_grad = jnp.zeros((RELATIONS, D), jnp.float32)
    for round_idx in range(ROUNDS):
        flip_mask = N_DOM // 2 if round_idx == 0 else 1
        partner = np.arange(N_DOM) ^ flip_mask
        partner_slabs = slabs[partner]

        def one_bucket(carried, inputs):
            own_slab, other_slab, source_list, kind_list, target_list, counts, negatives = inputs
            live_mask = (positions < counts[slot_of]).astype(jnp.float32)
            grad_source, grad_target, d_rel = edge_terms(own_slab, other_slab, relations, source_list, kind_list, target_list, live_mask, negatives)
            return (carried.at[kind_list].add(d_rel), (grad_source, grad_target))
        rel_grad, (grad_sources, grad_targets) = lax.scan(one_bucket, rel_grad, (slabs, partner_slabs, src_rows[:, round_idx], rel_ids[:, round_idx], dst_rows[:, round_idx], live_count[:, round_idx], neg_rows[:, round_idx]))
        gradient = grad_sources + grad_targets[partner]
        states = states + lax.optimization_barrier(jnp.mean(gradient * gradient, axis=-1))
        slabs = slabs - LEARN_RATE * gradient / (jnp.sqrt(states)[..., None] + EPSILON)
    new_relation_state = relation_state + lax.optimization_barrier(jnp.mean(rel_grad * rel_grad, axis=-1))
    new_relations = relations - LEARN_RATE * rel_grad / (jnp.sqrt(new_relation_state)[:, None] + EPSILON)
    return (slabs.reshape(N_DOM * ROWS, D), states.reshape(N_DOM * ROWS), new_relations, new_relation_state)
```

```python
import functools

import jax
import jax.numpy as jnp
from jax import lax
from jax.experimental import pallas as pl
from jax.experimental.pallas import tpu as pltpu
from jax.sharding import Mesh, PartitionSpec as P

D = 400
HALF = 200
RELATIONS = 2560
NEG = 1024
ROUNDS = 2
CAP = 256
LIGHT = 64
SLOTS = 512
CHUNK = 128
ROWS = 256
QUARTER = RELATIONS // 4
KROWS = 2048
LEARN_RATE = 0.1
EPSILON = 1e-08
REL = ("l", "c")
SPREAD = ("y", "h")
F32, BF16, I32 = jnp.float32, jnp.bfloat16, jnp.int32
VMEM = pl.BlockSpec(memory_space=pltpu.VMEM)
SMEM = pl.BlockSpec(memory_space=pltpu.SMEM)


def flip(block, axis, mask):
    count = lax.axis_size(axis)
    return lax.ppermute(block, axis, [(i, i ^ mask) for i in range(count)])


def split(value):
    high = value.astype(BF16)
    return high, (value - high.astype(F32)).astype(BF16)


def dot(first, second, over):
    return lax.dot_general(first, second, ((over[:1], over[1:]), ((), ())), preferred_element_type=F32)


def dot2(first, second, over):
    return dot(first[0], second, over) + dot(first[1], second, over)


def dot3(first, second, over):
    return dot(first[0], second[0], over) + (dot(first[0], second[1], over) + dot(first[1], second[0], over))


def places(rows, ids, base):
    return lax.broadcasted_iota(I32, (rows, ids.shape[-1]), 0) + base == ids


def hot(rows, ids, base):
    return jnp.where(places(rows, ids, base), 1.0, 0.0).astype(BF16)


def call(kernel, out_shape, in_specs, scratch, flops, moved, **more):
    return pl.pallas_call(
        kernel,
        out_shape=out_shape,
        in_specs=in_specs,
        scratch_shapes=scratch,
        compiler_params=pltpu.CompilerParams(vmem_limit_bytes=40 * 1024 * 1024),
        cost_estimate=pl.CostEstimate(flops=flops, bytes_accessed=moved, transcendentals=0),
        **more,
    )


def shape(*dims):
    return jax.ShapeDtypeStruct(dims, F32)


def lookup_kernel(q_ref, ids_ref, neg_ref, table_ref, out_ref, count_ref, high_ref, low_ref):
    @pl.when(pl.program_id(0) == 0)
    def _():
        high_ref[...], low_ref[...] = split(table_ref[...])

    ids = ids_ref[0]
    total = jnp.zeros((D, SLOTS), F32)
    for part in range(RELATIONS // 512):
        at = slice(512 * part, 512 * part + 512)
        total += dot2((high_ref[:, at], low_ref[:, at]), hot(512, ids, 512 * part), (1, 0))
    out_ref[0] = total
    hits = jnp.where(places(ROWS, neg_ref[0], ROWS * q_ref[0]), 1.0, 0.0)
    count_ref[0] = jnp.sum(hits, axis=1, keepdims=True)


def lookup(q, ids, negatives, table):
    return call(
        lookup_kernel,
        [shape(ROUNDS, D, SLOTS), shape(ROUNDS, ROWS, 1)],
        [
            SMEM,
            pl.BlockSpec((1, 1, SLOTS), lambda t: (t, 0, 0)),
            pl.BlockSpec((1, 1, NEG), lambda t: (t, 0, 0)),
            pl.BlockSpec((D, RELATIONS), lambda t: (0, 0)),
        ],
        [pltpu.VMEM((D, RELATIONS), BF16)] * 2,
        2 * 2 * 2 * D * RELATIONS * SLOTS,
        8 * 1024 * 1024,
        grid=(ROUNDS,),
        out_specs=[
            pl.BlockSpec((1, D, SLOTS), lambda t: (t, 0, 0)),
            pl.BlockSpec((1, ROWS, 1), lambda t: (t, 0, 0)),
        ],
    )(q, ids, negatives, table)


def score_kernel(q_ref, ids_ref, near_ref, far_ref, rel_ref, count_ref, own_ref, back_ref, grad_ref, head_ref, kind_ref, high_ref, low_ref, h_ref, a_ref):
    q = q_ref[0]
    for k in range(4):
        for ref, at in ((near_ref, 256 * k), (far_ref, 256 * k + 128)):
            high_ref[:, at : at + 128], low_ref[:, at : at + 128] = split(ref[k])
    a_ref[...] = dot2((high_ref[...], low_ref[...]), hot(1024, ids_ref[0:1, :], 0), (1, 0))
    a1, a2 = a_ref[:HALF, :], a_ref[HALF:, :]
    w1, w2 = rel_ref[0, :HALF, :], rel_ref[0, HALF:, :]
    h_ref[:HALF, :] = a1 * w1 - a2 * w2
    h_ref[HALF:, :] = a1 * w2 + a2 * w1
    product = split(h_ref[...])
    own = split(own_ref[...])
    scores = dot3(own, product, (0, 0))
    small = jnp.exp(-jnp.abs(scores))
    larger = 1.0 / (1.0 + small)
    smaller = small * larger
    rising = scores >= 0
    target = ids_ref[2:3, :]
    live = jnp.where(target >= 0, 1.0 / NEG, 0.0)
    weight = jnp.where(rising, larger, smaller) * count_ref[0] * live
    weight -= jnp.where(places(ROWS, target, ROWS * q), jnp.where(rising, smaller, larger), 0.0)
    weight = split(weight)
    d_product = dot3(own, weight, (1, 0))
    for k in range(4):
        back_ref[k] = d_product[:, CHUNK * k : CHUNK * k + CHUNK]
    grad_ref[...] = dot3(product, weight, (1, 1))
    mine = pl.ds(pl.multiple_of(CHUNK * q, CHUNK), CHUNK)
    head_ref[...] = a_ref[:, mine]
    kind_ref[...] = rel_ref[0, :, mine]


def score(q, ids, near, far, rel_rows, counts, own, round_idx):
    return call(
        score_kernel,
        [shape(4, D, CHUNK), shape(D, ROWS), shape(D, CHUNK), shape(D, CHUNK)],
        [
            SMEM,
            pl.BlockSpec((4, SLOTS), lambda i: (0, 0)),
            pl.BlockSpec((4, D, CHUNK), lambda i: (0, 0, 0)),
            pl.BlockSpec((4, D, CHUNK), lambda i: (0, 0, 0)),
            pl.BlockSpec((1, D, SLOTS), lambda i: (round_idx, 0, 0)),
            pl.BlockSpec((1, ROWS, 1), lambda i: (round_idx, 0, 0)),
            pl.BlockSpec((D, ROWS), lambda i: (0, 0)),
        ],
        [pltpu.VMEM((D, 1024), BF16)] * 2 + [pltpu.VMEM((D, SLOTS), F32)] * 2,
        2 * 1024 * 1024 * 1024,
        8 * 1024 * 1024,
        grid=(1,),
        out_specs=[
            pl.BlockSpec((4, D, CHUNK), lambda i: (0, 0, 0)),
            pl.BlockSpec((D, ROWS), lambda i: (0, 0)),
            pl.BlockSpec((D, CHUNK), lambda i: (0, 0)),
            pl.BlockSpec((D, CHUNK), lambda i: (0, 0)),
        ],
    )(q, ids, near, far, rel_rows, counts, own)


def back_kernel(parts_ref, head_ref, kind_ref, d_head_ref, d_kind_ref):
    up = (parts_ref[0] + parts_ref[1]) + (parts_ref[2] + parts_ref[3])
    u1, u2 = up[:HALF, :], up[HALF:, :]
    for other_ref, out_ref in ((kind_ref, d_head_ref), (head_ref, d_kind_ref)):
        o1, o2 = other_ref[:HALF, :], other_ref[HALF:, :]
        out_ref[:HALF, :] = u1 * o1 + u2 * o2
        out_ref[HALF:, :] = u2 * o1 - u1 * o2


def back(parts, head, kind):
    return call(
        back_kernel,
        [shape(D, CHUNK)] * 2,
        [VMEM] * 3,
        [],
        10 * D * CHUNK,
        8 * D * CHUNK * 4,
        out_specs=[VMEM] * 2,
    )(parts, head, kind)


def gather_parts(parts_ref, high_ref, low_ref):
    for k in range(4):
        at = slice(CHUNK * k, CHUNK * k + CHUNK)
        high_ref[:, at], low_ref[:, at] = split(parts_ref[k])


def update_kernel(q_ref, ids_ref, parts_ref, grad_ref, own_ref, state_ref, out_ref, out_state_ref, high_ref, low_ref):
    gather_parts(parts_ref, high_ref, low_ref)
    spots = hot(ROWS, ids_ref[3:4, :], ROWS * q_ref[0])
    gradient = grad_ref[...] + dot2((high_ref[...], low_ref[...]), spots, (1, 1))
    state = state_ref[...] + jnp.sum(gradient * gradient, axis=0, keepdims=True) * (1.0 / D)
    out_state_ref[...] = state
    out_ref[...] = own_ref[...] - gradient * (LEARN_RATE / (jnp.sqrt(state) + EPSILON))


def update(q, ids, parts, grad, own, state):
    return call(
        update_kernel,
        [shape(D, ROWS), shape(1, ROWS)],
        [SMEM] + [VMEM] * 5,
        [pltpu.VMEM((D, SLOTS), BF16)] * 2,
        2 * 2 * D * SLOTS * ROWS,
        2 * 1024 * 1024,
        out_specs=[VMEM] * 2,
    )(q, ids, parts, grad, own, state)


def kinds_kernel(first, q_ref, ids_ref, parts_ref, *refs):
    out_ref, high_ref, low_ref = refs[-3:]
    gather_parts(parts_ref, high_ref, low_ref)
    spots = hot(QUARTER, ids_ref[1:2, :], QUARTER * q_ref[0])
    total = dot2((high_ref[...], low_ref[...]), spots, (1, 1))
    for k in range(5):
        at = slice(D * k, D * k + D)
        tile = total[:, 128 * k : 128 * k + 128]
        out_ref[at, :] = tile if first else refs[0][at, :] + tile
    out_ref[5 * D :, :] = jnp.zeros((KROWS - 5 * D, 128), F32)


def kinds(q, ids, parts, before):
    more = [] if before is None else [before]
    return call(
        functools.partial(kinds_kernel, before is None),
        shape(KROWS, 128),
        [SMEM] + [VMEM] * (2 + len(more)),
        [pltpu.VMEM((D, SLOTS), BF16)] * 2,
        2 * 2 * D * SLOTS * QUARTER,
        3 * 1024 * 1024,
        out_specs=VMEM,
    )(q, ids, parts, *more)


def relations_kernel(q_ref, *refs):
    grads, (table_ref, state_ref, out_ref, out_state_ref) = refs[:4], refs[4:]
    for d in range(4):

        @pl.when(pl.program_id(0) == d)
        def _():
            for k in range(5):
                at = slice(128 * k, 128 * k + 128)
                gradient = grads[d][D * k : D * k + D, :]
                state = state_ref[:, at] + jnp.sum(gradient * gradient, axis=0, keepdims=True) * (1.0 / D)
                out_state_ref[:, at] = state
                out_ref[:, at] = table_ref[:, at] - gradient * (LEARN_RATE / (jnp.sqrt(state) + EPSILON))


def update_relations(q, grads, table, state):
    mine = lambda d, q: (0, d ^ q[0])
    whole = lambda d, q: (0, 0)
    return pl.pallas_call(
        relations_kernel,
        out_shape=[shape(D, RELATIONS), shape(1, RELATIONS)],
        grid_spec=pltpu.PrefetchScalarGridSpec(
            num_scalar_prefetch=1,
            grid=(4,),
            in_specs=[pl.BlockSpec((KROWS, 128), whole)] * 4
            + [pl.BlockSpec((D, QUARTER), mine), pl.BlockSpec((1, QUARTER), mine)],
            out_specs=[pl.BlockSpec((D, QUARTER), mine), pl.BlockSpec((1, QUARTER), mine)],
        ),
        compiler_params=pltpu.CompilerParams(vmem_limit_bytes=40 * 1024 * 1024),
        cost_estimate=pl.CostEstimate(flops=10 * D * RELATIONS, bytes_accessed=12 * 1024 * 1024, transcendentals=0),
    )(q, *grads, table, state)


def exchange_lists(src_rows, rel_ids, dst_rows, live_count, neg_rows):
    live = jnp.arange(CAP, dtype=I32)[None, :] < live_count[0]
    lists = jnp.where(live[:, None, :], jnp.stack([src_rows[0], rel_ids[0], dst_rows[0]], axis=1), -1)
    negatives, worked = [], []
    for t, (axis, mask) in enumerate((("z", 8), ("h", 1))):
        sent = jnp.concatenate([lists[t].reshape(6, 128), neg_rows[0, t].reshape(8, 128)], axis=0)
        got = flip(sent, axis, mask)
        worked.append(got[:6])
        negatives.append(got[6:].reshape(1, NEG))
    mine = jnp.concatenate(worked + [lists[:, 0].reshape(4, 128)], axis=0)
    every = lax.all_gather(mine, REL, axis=0).reshape(4, 8, CAP)
    light = jnp.moveaxis(every[:, :, :LIGHT], 0, 1).reshape(8, 4 * LIGHT)
    heavy = jnp.max(every[:, :, LIGHT:], axis=0)
    slots = jnp.concatenate([light, heavy, jnp.full((8, SLOTS - 4 * LIGHT - (CAP - LIGHT)), -1, I32)], axis=1)
    ids = [jnp.concatenate([slots[3 * t : 3 * t + 3], slots[6 + t : 7 + t]], axis=0) for t in range(ROUNDS)]
    return ids, jnp.stack(negatives)


def local(entities, entity_state, relations, relation_state, src_rows, rel_ids, dst_rows, live_count, neg_rows):
    q = lax.axis_index(REL).astype(I32).reshape(1)
    own, state = entities.T, entity_state.reshape(1, ROWS)
    table = relations.T
    ids, negatives = exchange_lists(src_rows, rel_ids, dst_rows, live_count, neg_rows)
    rel_rows, counts = lookup(q, jnp.stack([ids[0][1:2], ids[1][1:2]]), negatives, table)
    total = None
    for t, (axis, mask) in enumerate((("z", 8), ("h", 1))):
        near = lax.all_gather(flip(own[:, :128], axis, mask), REL, axis=0)
        far = lax.all_gather(flip(own[:, 128:], axis, mask), REL, axis=0)
        parts, grad, head, kind = score(q, ids[t], near, far, rel_rows, counts, own, t)
        parts = lax.all_to_all(parts, REL, 0, 0)
        d_head, d_kind = back(parts, head, kind)
        d_heads = lax.all_gather(flip(d_head, axis, mask), REL, axis=0)
        own, state = update(q, ids[t], d_heads, grad, own, state)
        total = kinds(q, ids[t], lax.all_gather(d_kind, REL, axis=0), total)
    shares = lax.all_to_all(total.reshape(8, 256, 128), SPREAD, 0, 0)
    share = jnp.sum(shares, axis=0)
    pieces = lax.all_to_all(share.reshape(16, 16, 128), "z", 0, 0)
    piece = jnp.sum(pieces, axis=0)
    share = lax.all_to_all(jnp.broadcast_to(piece[None], (16, 16, 128)), "z", 0, 0).reshape(256, 128)
    whole = lax.all_to_all(jnp.broadcast_to(share[None], (8, 256, 128)), SPREAD, 0, 0).reshape(KROWS, 128)
    across = flip(whole, "l", 1)
    grads = [whole, flip(whole, "c", 1), across, flip(across, "c", 1)]
    new_table, new_table_state = update_relations(q, grads, table, relation_state.reshape(1, RELATIONS))
    return own.T, state.reshape(ROWS), new_table.T, new_table_state.reshape(RELATIONS)


def solution(mesh):
    fine = Mesh(mesh.devices.reshape(16, 4, 2, 2, 2), ("z", "y", "h", "l", "c"))
    dom, rel = ("z", "y", "h"), REL
    edge = P(dom, None, rel)
    in_specs = (P(dom + rel, None), P(dom + rel), P(), P(), edge, edge, edge, edge, P(dom, None, None))
    out_specs = (P(dom + rel, None), P(dom + rel), P(), P())
    return jax.shard_map(local, mesh=fine, in_specs=in_specs, out_specs=out_specs, check_vma=False)
```

```python
import functools

import jax
import jax.numpy as jnp
from jax import lax
from jax.experimental import pallas as pl
from jax.experimental.pallas import tpu as pltpu
from jax.sharding import Mesh, PartitionSpec as P

D = 400
HALF = 200
RELATIONS = 2560
NEG = 1024
CAP = 256
LIGHT = 64
SLOTS = 512
PAIR = 256
CHUNK = 128
ROWS = 256
QUARTER = RELATIONS // 4
PART = 512
KROWS = 2048
LETTER = D + 16
LEARN_RATE = 0.1
EPSILON = 1e-08
REL = ("l", "c")
SPREAD = ("y", "h")
F32, BF16, I32 = jnp.float32, jnp.bfloat16, jnp.int32
SMEM = pl.BlockSpec(memory_space=pltpu.SMEM)
tied = lax.optimization_barrier


def flip(block, axis, mask=1):
    count = lax.axis_size(axis)
    return lax.ppermute(block, axis, [(i, i ^ mask) for i in range(count)])


def split(value):
    high = value.astype(BF16)
    return high, (value - high.astype(F32)).astype(BF16)


def dot(first, second, over):
    return lax.dot_general(first, second, ((over[:1], over[1:]), ((), ())), preferred_element_type=F32)


def dot2(first, second, over):
    return dot(first[0], second, over) + dot(first[1], second, over)


def dot3(first, second, over):
    return dot(first[0], second[0], over) + (dot(first[0], second[1], over) + dot(first[1], second[0], over))


def places(rows, ids, base):
    return lax.broadcasted_iota(I32, (rows, ids.shape[-1]), 0) + base == ids


def hot(rows, ids, base):
    return jnp.where(places(rows, ids, base), 1.0, 0.0).astype(BF16)


def times(out_ref, at, a1, a2, w1, w2):
    out_ref[:HALF, at] = a1 * w1 - a2 * w2
    out_ref[HALF:D, at] = a1 * w2 + a2 * w1


def back(out_ref, at, u1, u2, o1, o2):
    out_ref[:HALF, at] = u1 * o1 + u2 * o2
    out_ref[HALF:D, at] = u2 * o1 - u1 * o2


def shape(*dims):
    return jax.ShapeDtypeStruct(dims, F32)


def whole(*dims):
    return pl.BlockSpec(dims, lambda *_: (0,) * len(dims))


def call(kernel, out_shape, in_specs, out_specs, scratch, flops, moved, grid=(1,), room=40, **more):
    return pl.pallas_call(
        kernel,
        out_shape=out_shape,
        grid_spec=pltpu.PrefetchScalarGridSpec(
            num_scalar_prefetch=1, grid=grid, in_specs=in_specs, out_specs=out_specs, scratch_shapes=scratch
        ),
        compiler_params=pltpu.CompilerParams(vmem_limit_bytes=room * 1024 * 1024),
        cost_estimate=pl.CostEstimate(flops=flops, bytes_accessed=moved, transcendentals=0),
        **more,
    )


def lookup_kernel(s_ref, ids_ref, table_ref, out_ref):
    step = pl.program_id(0)
    table = split(table_ref[...])
    for k in range(ids_ref.shape[0]):
        found = dot2(table, hot(PART, ids_ref[k], PART * step), (1, 0))

        @pl.when(step == 0)
        def _():
            out_ref[k] = found

        @pl.when(step > 0)
        def _():
            out_ref[k] += found


def lookup(s, ids, table):
    lists, _, width = ids.shape
    return call(
        lookup_kernel,
        shape(lists, D, width),
        [whole(lists, 1, width), pl.BlockSpec((D, PART), lambda i, s: (0, i))],
        whole(lists, D, width),
        [],
        4 * D * RELATIONS * lists * width,
        5 * 1024 * 1024,
        grid=(RELATIONS // PART,),
        room=56,
    )(s, ids, table)


def chunk_rows(q, ids, near_ref, far_ref):
    first = q & 2
    total = jnp.zeros((D, CHUNK), F32)
    for ref, base in ((near_ref, first), (far_ref, first ^ 2)):
        for k in range(2):
            total += dot2(split(ref[k]), hot(ROWS, ids, ROWS * (base + k)), (1, 0))
    return total


def heads_kernel(s_ref, ids_ref, near_ref, far_ref, out_ref):
    out_ref[...] = chunk_rows(s_ref[0], ids_ref[...], near_ref, far_ref)


def letter_kernel(s_ref, ids_ref, near_ref, far_ref, rel_ref, target_ref, neg_ref, head_ref, out_ref):
    head_ref[...] = chunk_rows(s_ref[0], ids_ref[...], near_ref, far_ref)
    every = slice(None)
    times(out_ref, every, head_ref[:HALF, :], head_ref[HALF:, :], rel_ref[0, :HALF, :], rel_ref[0, HALF:, :])
    out_ref[D : D + 8, :] = jnp.broadcast_to(target_ref[...], (8, CHUNK)).astype(F32)
    out_ref[D + 8 :, :] = neg_ref[...].astype(F32)


HEADS_IN = [whole(1, CHUNK), whole(2, D, ROWS), whole(2, D, ROWS)]
HEADS_COST = (4 * D * 1024 * CHUNK, 2 * 1024 * 1024)


def heads(s, ids, near, far):
    return call(heads_kernel, shape(D, CHUNK), HEADS_IN, whole(D, CHUNK), [], *HEADS_COST)(s, ids, near, far)


def letter(s, ids, near, far, rel_rows, target, negatives):
    return call(
        letter_kernel,
        [shape(D, CHUNK), shape(LETTER, CHUNK)],
        HEADS_IN + [whole(1, D, CHUNK), whole(1, CHUNK), whole(8, 128)],
        [whole(D, CHUNK), whole(LETTER, CHUNK)],
        [],
        *HEADS_COST,
    )(s, ids, near, far, rel_rows, target, negatives)


def weigh(s_ref, h_ref, target, negatives, own_ref, other_ref, keep_ref, send_ref, grad_ref, grad_send_ref):
    q = s_ref[0]
    product = split(h_ref[...])
    live = jnp.where(target >= 0, 1.0 / NEG, 0.0)
    d_product = jnp.zeros((D, PAIR), F32)
    for k, (ref, out_ref) in enumerate(((own_ref, grad_ref), (other_ref, grad_send_ref))):
        base = ROWS * (q ^ (2 * k))
        hits = jnp.zeros((ROWS, 128), F32)
        for row in range(8):
            hits += jnp.where(places(ROWS, negatives[row : row + 1, :], base), 1.0, 0.0)
        rows = split(ref[...])
        scores = dot3(rows, product, (0, 0))
        small = jnp.exp(-jnp.abs(scores))
        larger = 1.0 / (1.0 + small)
        smaller = small * larger
        rising = scores >= 0
        weight = jnp.where(rising, larger, smaller) * jnp.sum(hits, axis=1, keepdims=True) * live
        weight -= jnp.where(places(ROWS, target, base), jnp.where(rising, smaller, larger), 0.0)
        weight = split(weight)
        d_product += dot3(rows, weight, (1, 0))
        out_ref[...] = dot3(product, weight, (1, 1))
    h_ref[...] = d_product
    core = q & 1
    keep_ref[...] = h_ref[:, pl.ds(pl.multiple_of(CHUNK * core, CHUNK), CHUNK)]
    send_ref[...] = h_ref[:, pl.ds(pl.multiple_of(CHUNK * (1 - core), CHUNK), CHUNK)]


def answer_kernel(s_ref, letters_ref, own_ref, other_ref, keep_ref, send_ref, grad_ref, grad_send_ref, h_ref):
    for k in range(2):
        h_ref[:, CHUNK * k : CHUNK * k + CHUNK] = letters_ref[k, :D, :]
    target = jnp.concatenate([letters_ref[k, D : D + 1, :] for k in range(2)], axis=1).astype(I32)
    negatives = letters_ref[0, D + 8 :, :].astype(I32)
    weigh(s_ref, h_ref, target, negatives, own_ref, other_ref, keep_ref, send_ref, grad_ref, grad_send_ref)


def answer(s, letters, own, other):
    return call(
        answer_kernel,
        [shape(D, CHUNK)] * 2 + [shape(D, ROWS)] * 2,
        [whole(2, LETTER, CHUNK), whole(D, ROWS), whole(D, ROWS)],
        [whole(D, CHUNK)] * 2 + [whole(D, ROWS)] * 2,
        [pltpu.VMEM((D, PAIR), F32)],
        1024 * 1024 * 1024,
        5 * 1024 * 1024,
    )(s, letters, own, other)


def score_kernel(s_ref, target_ref, neg_ref, a_ref, rel_ref, own_ref, other_ref, keep_ref, send_ref, grad_ref, grad_send_ref, head_ref, kind_ref, h_ref):
    first = s_ref[1]
    for k in range(2):
        at = slice(CHUNK * k, CHUNK * k + CHUNK)
        a1, a2 = a_ref[first + k, :HALF, :], a_ref[first + k, HALF:, :]
        times(h_ref, at, a1, a2, rel_ref[0, :HALF, at], rel_ref[0, HALF:, at])
    weigh(s_ref, h_ref, target_ref[...], neg_ref[...], own_ref, other_ref, keep_ref, send_ref, grad_ref, grad_send_ref)
    core = s_ref[0] & 1
    head_ref[...] = a_ref[first + core]
    kind_ref[...] = rel_ref[0, :, pl.ds(pl.multiple_of(CHUNK * core, CHUNK), CHUNK)]


def score(s, target, negatives, head_rows, rel_rows, own, other):
    return call(
        score_kernel,
        [shape(D, CHUNK)] * 2 + [shape(D, ROWS)] * 2 + [shape(D, CHUNK)] * 2,
        [
            whole(1, PAIR),
            whole(8, 128),
            whole(4, D, CHUNK),
            whole(1, D, PAIR),
            whole(D, ROWS),
            whole(D, ROWS),
        ],
        [whole(D, CHUNK)] * 2 + [whole(D, ROWS)] * 2 + [whole(D, CHUNK)] * 2,
        [pltpu.VMEM((D, PAIR), F32)],
        1024 * 1024 * 1024,
        5 * 1024 * 1024,
    )(s, target, negatives, head_rows, rel_rows, own, other)


def back_kernel(s_ref, keep_ref, got_ref, head_ref, kind_ref, d_head_ref, d_kind_ref):
    up = keep_ref[...] + got_ref[...]
    for other_ref, out_ref in ((kind_ref, d_head_ref), (head_ref, d_kind_ref)):
        back(out_ref, slice(None), up[:HALF, :], up[HALF:, :], other_ref[:HALF, :], other_ref[HALF:, :])


def chunk_back(s, keep, got, head, kind):
    chunk = whole(D, CHUNK)
    return call(back_kernel, [shape(D, CHUNK)] * 2, [chunk] * 4, [chunk] * 2, [], 10 * D * CHUNK, 32 * D * CHUNK)(
        s, keep, got, head, kind
    )


def step_rows(gradient, own_ref, state_ref, out_ref, out_state_ref):
    state = state_ref[...] + jnp.sum(gradient * gradient, axis=0, keepdims=True) * (1.0 / D)
    out_state_ref[...] = state
    out_ref[...] = own_ref[...] - gradient * (LEARN_RATE / (jnp.sqrt(state) + EPSILON))


def chunk_at(k):
    return slice(CHUNK * k, CHUNK * k + CHUNK)


def answered_kernel(s_ref, ids_ref, answers_ref, rel_ref, grad_ref, got_ref, own_ref, state_ref, out_ref, out_state_ref, high_ref, low_ref, d_ref):
    for k in range(4):
        at = chunk_at(k % 2)
        w1, w2 = rel_ref[k // 2, :HALF, at], rel_ref[k // 2, HALF:, at]
        back(d_ref, slice(None), answers_ref[k, :HALF, :], answers_ref[k, HALF:, :], w1, w2)
        high_ref[:, chunk_at(k)], low_ref[:, chunk_at(k)] = split(d_ref[...])
    spots = hot(ROWS, ids_ref[...], ROWS * s_ref[0])
    gradient = grad_ref[...] + got_ref[...] + dot2((high_ref[...], low_ref[...]), spots, (1, 1))
    step_rows(gradient, own_ref, state_ref, out_ref, out_state_ref)


ROWS_SPECS = [whole(D, ROWS), whole(1, ROWS)]
PARTS = [pltpu.VMEM((D, SLOTS), BF16)] * 2


def update_answered(s, ids, answers, rel_rows, grad, got, own, state):
    return call(
        answered_kernel,
        [shape(D, ROWS), shape(1, ROWS)],
        [whole(1, SLOTS), whole(4, D, CHUNK), whole(2, D, PAIR), whole(D, ROWS), whole(D, ROWS)] + ROWS_SPECS,
        ROWS_SPECS,
        PARTS + [pltpu.VMEM((D, CHUNK), F32)],
        4 * D * SLOTS * ROWS,
        4 * 1024 * 1024,
    )(s, ids, answers, rel_rows, grad, got, own, state)


def join_kernel(s_ref, ids_ref, parts_ref, grad_ref, send_ref, out_ref, out_send_ref):
    parts = [split(parts_ref[k]) for k in range(2)]
    for flipped, ref, to_ref in ((0, grad_ref, out_ref), (2, send_ref, out_send_ref)):
        base = ROWS * (s_ref[0] ^ flipped)
        total = ref[...]
        for k in range(2):
            total += dot2(parts[k], hot(ROWS, ids_ref[:, chunk_at(k)], base), (1, 1))
        to_ref[...] = total


def join(s, ids, parts, grad, grad_send):
    return call(
        join_kernel,
        [shape(D, ROWS)] * 2,
        [whole(1, PAIR), whole(2, D, CHUNK), whole(D, ROWS), whole(D, ROWS)],
        [whole(D, ROWS)] * 2,
        [],
        4 * D * PAIR * 2 * ROWS,
        3 * 1024 * 1024,
    )(s, ids, parts, grad, grad_send)


def update_kernel(s_ref, grad_ref, got_ref, own_ref, state_ref, out_ref, out_state_ref):
    step_rows(grad_ref[...] + got_ref[...], own_ref, state_ref, out_ref, out_state_ref)


def update(s, grad, got, own, state):
    ins = [whole(D, ROWS)] * 2 + ROWS_SPECS
    return call(update_kernel, [shape(D, ROWS), shape(1, ROWS)], ins, ROWS_SPECS, [], 8 * D * ROWS, 16 * D * ROWS)(
        s, grad, got, own, state
    )


def count_in(s_ref, ids_ref, before_ref, out_ref, high_ref, low_ref):
    spots = hot(QUARTER, ids_ref[...], QUARTER * s_ref[0])
    total = dot2((high_ref[...], low_ref[...]), spots, (1, 1))
    for k in range(5):
        at = slice(D * k, D * k + D)
        tile = total[:, 128 * k : 128 * k + 128]
        out_ref[at, :] = tile if before_ref is None else before_ref[at, :] + tile
    out_ref[5 * D :, :] = jnp.zeros((KROWS - 5 * D, 128), F32)


def kinds_answered_kernel(s_ref, ids_ref, answers_ref, heads_ref, out_ref, high_ref, low_ref, d_ref):
    for k in range(4):
        a1, a2 = heads_ref[k, :HALF, :], heads_ref[k, HALF:, :]
        back(d_ref, slice(None), answers_ref[k, :HALF, :], answers_ref[k, HALF:, :], a1, a2)
        high_ref[:, chunk_at(k)], low_ref[:, chunk_at(k)] = split(d_ref[...])
    count_in(s_ref, ids_ref, None, out_ref, high_ref, low_ref)


def kinds_kernel(s_ref, ids_ref, parts_ref, before_ref, out_ref, high_ref, low_ref):
    for k in range(4):
        high_ref[:, chunk_at(k)], low_ref[:, chunk_at(k)] = split(parts_ref[k])
    count_in(s_ref, ids_ref, before_ref, out_ref, high_ref, low_ref)


KINDS_COST = (4 * D * SLOTS * QUARTER, 3 * 1024 * 1024)


def kinds_answered(s, ids, answers, heads):
    ins = [whole(1, SLOTS)] + [whole(4, D, CHUNK)] * 2
    scratch = PARTS + [pltpu.VMEM((D, CHUNK), F32)]
    return call(kinds_answered_kernel, shape(KROWS, 128), ins, whole(KROWS, 128), scratch, *KINDS_COST)(
        s, ids, answers, heads
    )


def kinds(s, ids, parts, before):
    ins = [whole(1, SLOTS), whole(4, D, CHUNK), whole(KROWS, 128)]
    return call(kinds_kernel, shape(KROWS, 128), ins, whole(KROWS, 128), PARTS, *KINDS_COST)(s, ids, parts, before)


def relations_kernel(core_ref, grad_ref, table_ref, state_ref, *refs):
    out_ref, out_state_ref = refs[-2:]
    for k in range(5):
        at = slice(128 * k, 128 * k + 128)
        gradient = grad_ref[0, D * k : D * k + D, :]
        state = state_ref[:, at] + jnp.sum(gradient * gradient, axis=0, keepdims=True) * (1.0 / D)
        out_state_ref[:, at] = state
        out_ref[:, at] = table_ref[:, at] - gradient * (LEARN_RATE / (jnp.sqrt(state) + EPSILON))


def update_relations(core, grads, table, state, before):
    mine = lambda l, core: (0, 2 * l + core[0])
    blocks = [pl.BlockSpec((D, QUARTER), mine), pl.BlockSpec((1, QUARTER), mine)]
    return call(
        relations_kernel,
        [shape(D, RELATIONS), shape(1, RELATIONS)],
        [pl.BlockSpec((1, KROWS, 128), lambda l, core: (l, 0, 0))] + blocks + [pl.BlockSpec(memory_space=pl.ANY)] * len(before),
        blocks,
        [],
        5 * D * RELATIONS,
        6 * 1024 * 1024,
        grid=(2,),
        room=56,
        input_output_aliases={4: 0, 5: 1} if before else {},
    )(core, grads, table, state, *before)


def slot_lists(src_rows, rel_ids, dst_rows, live_count):
    live = jnp.arange(CAP, dtype=I32)[None, :] < live_count[0]
    lists = jnp.where(live[:, None, :], jnp.stack([src_rows[0], rel_ids[0], dst_rows[0]], axis=1), -1)
    every = lax.all_gather(lists.reshape(12, 128), REL, axis=0).reshape(4, 6, CAP)
    light = jnp.moveaxis(every[:, :, :LIGHT], 0, 1).reshape(6, 4 * LIGHT)
    heavy = jnp.max(every[:, :, LIGHT:], axis=0)
    empty = jnp.full((6, SLOTS - 4 * LIGHT - (CAP - LIGHT)), -1, I32)
    return jnp.concatenate([light, heavy, empty], axis=1)


def local(entities, entity_state, relations, relation_state, src_rows, rel_ids, dst_rows, live_count, neg_rows):
    place = lax.axis_index(REL).astype(I32)
    core, chip, side = place & 1, place // 2, lax.axis_index("h").astype(I32)
    s = place.reshape(1)
    own, state = entities.T, entity_state.reshape(1, ROWS)
    table = relations.T
    pick = lambda lists, rows, at: lax.dynamic_slice_in_dim(lists.reshape(rows, -1), at, 1, 0)

    slots = slot_lists(src_rows, rel_ids, dst_rows, live_count)
    own, slots = tied((own, slots))
    other = flip(own, "l")
    near = lax.all_gather(own, "c", axis=0)
    chunk_ids, chunk_kinds, chunk_targets = [pick(slots[k], 4, place) for k in range(3)]
    chunk_rel = lookup(s, chunk_kinds[None], table)
    far = lax.all_gather(other, "c", axis=0)
    head, mail = letter(s, chunk_ids, near, far, chunk_rel, chunk_targets, neg_rows[0, 0].reshape(8, 128))
    mail, head, bucket_kinds = tied((mail, head, slots[1]))
    rel_rows = lookup(s, bucket_kinds.reshape(2, 1, PAIR), table)
    mail, head_rows, rel_rows = tied((flip(mail, "z", 8), lax.all_gather(head, REL, axis=0), rel_rows))
    keep, send, grad, grad_send = answer(s, lax.all_gather(mail, "c", axis=0), own, other)
    reply = keep + flip(send, "c")
    sent = jnp.concatenate([slots[4:6].reshape(8, 128), neg_rows[0, 1].reshape(8, 128)], axis=0)
    reply, sent = tied((reply, sent))
    got = flip(sent, "h")
    kind_ids, target_ids, negatives = got[:4].reshape(1, SLOTS), got[4:8], got[8:]
    later_rows = lookup(s, pick(kind_ids, 2, chip)[None], table)
    reply, grad_got, later_rows = tied((flip(reply, "z", 8), flip(grad_send, "l"), later_rows))
    answers = lax.all_gather(reply, REL, axis=0)
    own, state = update_answered(s, slots[0:1], answers, rel_rows, grad, grad_got, own, state)
    total = kinds_answered(s, slots[1:2], answers, head_rows)

    other = flip(own, "l")
    near = lax.all_gather(own, "c", axis=0)
    other, total = tied((other, total))
    chunk = heads(s, pick(slots[3], 4, place), near, lax.all_gather(other, "c", axis=0))
    head_rows = lax.all_gather(chunk, ("h", "c"), axis=0)
    beyond = jnp.stack([place, 2 * (1 - side)])
    keep, send, grad, grad_send, head, kind = score(beyond, pick(target_ids, 2, chip), negatives, head_rows, later_rows, own, other)
    d_head, d_kind = chunk_back(s, keep, flip(send, "c"), head, kind)
    d_kinds, d_head = tied((lax.all_gather(d_kind, REL, axis=0), flip(d_head, "h")))
    total = kinds(s, kind_ids, d_kinds, total)

    shares = lax.all_to_all(total.reshape(8, 256, 128), SPREAD, 0, 0)
    pieces = lax.all_to_all(jnp.sum(shares, axis=0).reshape(16, 16, 128), "z", 0, 0)
    grad, grad_send = join(s, pick(slots[3], 2, chip), lax.all_gather(d_head, "c", axis=0), grad, grad_send)
    pieces, grad, grad_send = tied((pieces, grad, grad_send))
    piece = jnp.sum(pieces, axis=0)
    share = lax.all_to_all(jnp.broadcast_to(piece[None], (16, 16, 128)), "z", 0, 0).reshape(256, 128)
    share, grad_got = tied((share, flip(grad_send, "l")))
    own, state = update(s, grad, grad_got, own, state)
    half = lax.all_to_all(jnp.broadcast_to(share[None], (16, 256, 128)), ("l",) + SPREAD, 0, 0).reshape(2, KROWS, 128)
    half, own, state = tied((half, own, state))
    table_state = relation_state.reshape(1, RELATIONS)
    first = update_relations(core.reshape(1), half, table, table_state, [])
    new_table, new_table_state = update_relations((1 - core).reshape(1), flip(half, "c"), table, table_state, first)
    return own.T, state.reshape(ROWS), new_table.T, new_table_state.reshape(RELATIONS)


def solution(mesh):
    fine = Mesh(mesh.devices.reshape(16, 4, 2, 2, 2), ("z", "y", "h", "l", "c"))
    dom, rel = ("z", "y", "h"), REL
    edge = P(dom, None, rel)
    in_specs = (P(dom + rel, None), P(dom + rel), P(), P(), edge, edge, edge, edge, P(dom, None, None))
    out_specs = (P(dom + rel, None), P(dom + rel), P(), P())
    return jax.shard_map(local, mesh=fine, in_specs=in_specs, out_specs=out_specs, check_vma=False)
```

```python
import functools

import jax
import jax.numpy as jnp
from jax import lax
from jax.experimental import pallas as pl
from jax.experimental.pallas import tpu as pltpu
from jax.sharding import Mesh, PartitionSpec as P

D = 400
HALF = 200
RELATIONS = 2560
NEG = 1024
CAP = 256
LIGHT = 64
SLOTS = 512
PAIR = 256
CHUNK = 128
USED = 112
SENT = 352
TAIL = D - SENT
ROWS = 256
QUARTER = RELATIONS // 4
PART = 512
KROWS = 2048
LETTER = SENT + 16
LEARN_RATE = 0.1
EPSILON = 1e-08
REL = ("l", "c")
SPREAD = ("y", "h")
F32, BF16, I32 = jnp.float32, jnp.bfloat16, jnp.int32
SMEM = pl.BlockSpec(memory_space=pltpu.SMEM)
tied = lax.optimization_barrier


def flip(block, axis, mask=1):
    count = lax.axis_size(axis)
    return lax.ppermute(block, axis, [(i, i ^ mask) for i in range(count)])


def split(value):
    high = value.astype(BF16)
    return high, (value - high.astype(F32)).astype(BF16)


def dot(first, second, over):
    return lax.dot_general(first, second, ((over[:1], over[1:]), ((), ())), preferred_element_type=F32)


def dot2(first, second, over):
    return dot(first[0], second, over) + dot(first[1], second, over)


def dot3(first, second, over):
    return dot(first[0], second[0], over) + (dot(first[0], second[1], over) + dot(first[1], second[0], over))


def places(rows, ids, base):
    return lax.broadcasted_iota(I32, (rows, ids.shape[-1]), 0) + base == ids


def hot(rows, ids, base):
    return jnp.where(places(rows, ids, base), 1.0, 0.0).astype(BF16)


def times(out_ref, at, a1, a2, w1, w2):
    out_ref[:HALF, at] = a1 * w1 - a2 * w2
    out_ref[HALF:D, at] = a1 * w2 + a2 * w1


def back(out_ref, at, u1, u2, o1, o2):
    out_ref[:HALF, at] = u1 * o1 + u2 * o2
    out_ref[HALF:D, at] = u2 * o1 - u1 * o2


def pack(out_ref, value):
    lanes = lax.broadcasted_iota(I32, (TAIL, CHUNK), 1)
    out_ref[:SENT, :] = value[:SENT, :]
    for group in range(USED // 16):
        at = slice(TAIL * group, TAIL * group + TAIL)
        moved = pltpu.roll(value[SENT:, :], (USED - 16 * group) % CHUNK, 1)
        out_ref[at, :] = jnp.where(lanes >= USED, moved, value[at, :])


def unpack(out_ref, at, value):
    lanes = lax.broadcasted_iota(I32, (TAIL, CHUNK), 1)
    out_ref[:SENT, at] = value
    rest = jnp.zeros((TAIL, CHUNK), F32)
    for group in range(USED // 16):
        moved = pltpu.roll(value[TAIL * group : TAIL * group + TAIL, :], (16 * group - USED) % CHUNK, 1)
        rest = jnp.where(lanes // 16 == group, moved, rest)
    out_ref[SENT:, at] = rest


EVERY = slice(None)
WORK = pltpu.VMEM((D, CHUNK), F32)


def shape(*dims):
    return jax.ShapeDtypeStruct(dims, F32)


def whole(*dims):
    return pl.BlockSpec(dims, lambda *_: (0,) * len(dims))


def call(kernel, out_shape, in_specs, out_specs, scratch, flops, moved, grid=(1,), room=40, **more):
    return pl.pallas_call(
        kernel,
        out_shape=out_shape,
        grid_spec=pltpu.PrefetchScalarGridSpec(
            num_scalar_prefetch=1, grid=grid, in_specs=in_specs, out_specs=out_specs, scratch_shapes=scratch
        ),
        compiler_params=pltpu.CompilerParams(vmem_limit_bytes=room * 1024 * 1024),
        cost_estimate=pl.CostEstimate(flops=flops, bytes_accessed=moved, transcendentals=0),
        **more,
    )


def lookup_kernel(s_ref, ids_ref, table_ref, out_ref):
    step = pl.program_id(0)
    table = split(table_ref[...])
    for k in range(ids_ref.shape[0]):
        found = dot2(table, hot(PART, ids_ref[k], PART * step), (1, 0))

        @pl.when(step == 0)
        def _():
            out_ref[k] = found

        @pl.when(step > 0)
        def _():
            out_ref[k] += found


def lookup(s, ids, table):
    lists, _, width = ids.shape
    return call(
        lookup_kernel,
        shape(lists, D, width),
        [whole(lists, 1, width), pl.BlockSpec((D, PART), lambda i, s: (0, i))],
        whole(lists, D, width),
        [],
        4 * D * RELATIONS * lists * width,
        5 * 1024 * 1024,
        grid=(RELATIONS // PART,),
        room=56,
    )(s, ids, table)


def chunk_rows(q, ids, near_ref, far_ref):
    first = q & 2
    total = jnp.zeros((D, CHUNK), F32)
    for ref, base in ((near_ref, first), (far_ref, first ^ 2)):
        for k in range(2):
            total += dot2(split(ref[k]), hot(ROWS, ids, ROWS * (base + k)), (1, 0))
    return total


def heads_kernel(s_ref, ids_ref, near_ref, far_ref, out_ref):
    pack(out_ref, chunk_rows(s_ref[0], ids_ref[...], near_ref, far_ref))


def letter_kernel(s_ref, ids_ref, near_ref, far_ref, rel_ref, target_ref, neg_ref, head_ref, out_ref, work_ref, a_ref):
    a_ref[...] = chunk_rows(s_ref[0], ids_ref[...], near_ref, far_ref)
    pack(head_ref, a_ref[...])
    times(work_ref, EVERY, a_ref[:HALF, :], a_ref[HALF:, :], rel_ref[0, :HALF, :], rel_ref[0, HALF:, :])
    pack(out_ref, work_ref[...])
    out_ref[SENT : SENT + 8, :] = jnp.broadcast_to(target_ref[...], (8, CHUNK)).astype(F32)
    out_ref[SENT + 8 :, :] = neg_ref[...].astype(F32)


HEADS_IN = [whole(1, CHUNK), whole(2, D, ROWS), whole(2, D, ROWS)]
HEADS_COST = (4 * D * 1024 * CHUNK, 2 * 1024 * 1024)


def heads(s, ids, near, far):
    return call(heads_kernel, shape(SENT, CHUNK), HEADS_IN, whole(SENT, CHUNK), [], *HEADS_COST)(s, ids, near, far)


def letter(s, ids, near, far, rel_rows, target, negatives):
    return call(
        letter_kernel,
        [shape(SENT, CHUNK), shape(LETTER, CHUNK)],
        HEADS_IN + [whole(1, D, CHUNK), whole(1, CHUNK), whole(8, 128)],
        [whole(SENT, CHUNK), whole(LETTER, CHUNK)],
        [WORK] * 2,
        *HEADS_COST,
    )(s, ids, near, far, rel_rows, target, negatives)


def weigh(s_ref, h_ref, target, negatives, own_ref, other_ref, keep_ref, send_ref, grad_ref, grad_send_ref):
    q = s_ref[0]
    product = split(h_ref[...])
    live = jnp.where(target >= 0, 1.0 / NEG, 0.0)
    d_product = jnp.zeros((D, PAIR), F32)
    for k, (ref, out_ref) in enumerate(((own_ref, grad_ref), (other_ref, grad_send_ref))):
        base = ROWS * (q ^ (2 * k))
        hits = jnp.zeros((ROWS, 128), F32)
        for row in range(8):
            hits += jnp.where(places(ROWS, negatives[row : row + 1, :], base), 1.0, 0.0)
        rows = split(ref[...])
        scores = dot3(rows, product, (0, 0))
        small = jnp.exp(-jnp.abs(scores))
        larger = 1.0 / (1.0 + small)
        smaller = small * larger
        rising = scores >= 0
        weight = jnp.where(rising, larger, smaller) * jnp.sum(hits, axis=1, keepdims=True) * live
        weight -= jnp.where(places(ROWS, target, base), jnp.where(rising, smaller, larger), 0.0)
        weight = split(weight)
        d_product += dot3(rows, weight, (1, 0))
        out_ref[...] = dot3(product, weight, (1, 1))
    h_ref[...] = d_product
    core = q & 1
    pack(keep_ref, h_ref[:, pl.ds(pl.multiple_of(CHUNK * core, CHUNK), CHUNK)])
    pack(send_ref, h_ref[:, pl.ds(pl.multiple_of(CHUNK * (1 - core), CHUNK), CHUNK)])


def answer_kernel(s_ref, letters_ref, own_ref, other_ref, keep_ref, send_ref, grad_ref, grad_send_ref, h_ref):
    for k in range(2):
        unpack(h_ref, slice(CHUNK * k, CHUNK * k + CHUNK), letters_ref[k, :SENT, :])
    target = jnp.concatenate([letters_ref[k, SENT : SENT + 1, :] for k in range(2)], axis=1).astype(I32)
    negatives = letters_ref[0, SENT + 8 :, :].astype(I32)
    weigh(s_ref, h_ref, target, negatives, own_ref, other_ref, keep_ref, send_ref, grad_ref, grad_send_ref)


def answer(s, letters, own, other):
    return call(
        answer_kernel,
        [shape(SENT, CHUNK)] * 2 + [shape(D, ROWS)] * 2,
        [whole(2, LETTER, CHUNK), whole(D, ROWS), whole(D, ROWS)],
        [whole(SENT, CHUNK)] * 2 + [whole(D, ROWS)] * 2,
        [pltpu.VMEM((D, PAIR), F32)],
        1024 * 1024 * 1024,
        5 * 1024 * 1024,
    )(s, letters, own, other)


def score_kernel(s_ref, target_ref, neg_ref, a_ref, rel_ref, own_ref, other_ref, keep_ref, send_ref, grad_ref, grad_send_ref, head_ref, kind_ref, h_ref, work_ref):
    first = s_ref[1]
    for k in range(2):
        at = slice(CHUNK * k, CHUNK * k + CHUNK)
        unpack(work_ref, at, a_ref[first + k])
        times(h_ref, at, work_ref[:HALF, at], work_ref[HALF:, at], rel_ref[0, :HALF, at], rel_ref[0, HALF:, at])
    weigh(s_ref, h_ref, target_ref[...], neg_ref[...], own_ref, other_ref, keep_ref, send_ref, grad_ref, grad_send_ref)
    core = s_ref[0] & 1
    mine = pl.ds(pl.multiple_of(CHUNK * core, CHUNK), CHUNK)
    head_ref[...] = work_ref[:, mine]
    kind_ref[...] = rel_ref[0, :, mine]


def score(s, target, negatives, head_rows, rel_rows, own, other):
    return call(
        score_kernel,
        [shape(SENT, CHUNK)] * 2 + [shape(D, ROWS)] * 2 + [shape(D, CHUNK)] * 2,
        [
            whole(1, PAIR),
            whole(8, 128),
            whole(4, SENT, CHUNK),
            whole(1, D, PAIR),
            whole(D, ROWS),
            whole(D, ROWS),
        ],
        [whole(SENT, CHUNK)] * 2 + [whole(D, ROWS)] * 2 + [whole(D, CHUNK)] * 2,
        [pltpu.VMEM((D, PAIR), F32)] * 2,
        1024 * 1024 * 1024,
        5 * 1024 * 1024,
    )(s, target, negatives, head_rows, rel_rows, own, other)


def back_kernel(s_ref, keep_ref, got_ref, head_ref, kind_ref, d_head_ref, d_kind_ref, up_ref, work_ref):
    unpack(up_ref, EVERY, keep_ref[...] + got_ref[...])
    for other_ref, out_ref in ((kind_ref, d_head_ref), (head_ref, d_kind_ref)):
        back(work_ref, EVERY, up_ref[:HALF, :], up_ref[HALF:, :], other_ref[:HALF, :], other_ref[HALF:, :])
        pack(out_ref, work_ref[...])


def chunk_back(s, keep, got, head, kind):
    sent, chunk = whole(SENT, CHUNK), whole(D, CHUNK)
    out = [shape(SENT, CHUNK)] * 2
    ins = [sent] * 2 + [chunk] * 2
    return call(back_kernel, out, ins, [sent] * 2, [WORK] * 2, 10 * D * CHUNK, 32 * D * CHUNK)(s, keep, got, head, kind)


def step_rows(gradient, own_ref, state_ref, out_ref, out_state_ref):
    state = state_ref[...] + jnp.sum(gradient * gradient, axis=0, keepdims=True) * (1.0 / D)
    out_state_ref[...] = state
    out_ref[...] = own_ref[...] - gradient * (LEARN_RATE / (jnp.sqrt(state) + EPSILON))


def chunk_at(k):
    return slice(CHUNK * k, CHUNK * k + CHUNK)


def answered_kernel(s_ref, ids_ref, answers_ref, rel_ref, grad_ref, got_ref, own_ref, state_ref, out_ref, out_state_ref, high_ref, low_ref, d_ref, up_ref):
    for k in range(4):
        at = chunk_at(k % 2)
        w1, w2 = rel_ref[k // 2, :HALF, at], rel_ref[k // 2, HALF:, at]
        unpack(up_ref, EVERY, answers_ref[k])
        back(d_ref, EVERY, up_ref[:HALF, :], up_ref[HALF:, :], w1, w2)
        high_ref[:, chunk_at(k)], low_ref[:, chunk_at(k)] = split(d_ref[...])
    spots = hot(ROWS, ids_ref[...], ROWS * s_ref[0])
    gradient = grad_ref[...] + got_ref[...] + dot2((high_ref[...], low_ref[...]), spots, (1, 1))
    step_rows(gradient, own_ref, state_ref, out_ref, out_state_ref)


ROWS_SPECS = [whole(D, ROWS), whole(1, ROWS)]
PARTS = [pltpu.VMEM((D, SLOTS), BF16)] * 2


def update_answered(s, ids, answers, rel_rows, grad, got, own, state):
    return call(
        answered_kernel,
        [shape(D, ROWS), shape(1, ROWS)],
        [whole(1, SLOTS), whole(4, SENT, CHUNK), whole(2, D, PAIR), whole(D, ROWS), whole(D, ROWS)] + ROWS_SPECS,
        ROWS_SPECS,
        PARTS + [WORK] * 2,
        4 * D * SLOTS * ROWS,
        4 * 1024 * 1024,
    )(s, ids, answers, rel_rows, grad, got, own, state)


def join_kernel(s_ref, ids_ref, parts_ref, grad_ref, send_ref, out_ref, out_send_ref, work_ref):
    for k in range(2):
        unpack(work_ref, chunk_at(k), parts_ref[k])
    parts = split(work_ref[...])
    for flipped, ref, to_ref in ((0, grad_ref, out_ref), (2, send_ref, out_send_ref)):
        base = ROWS * (s_ref[0] ^ flipped)
        to_ref[...] = ref[...] + dot2(parts, hot(ROWS, ids_ref[...], base), (1, 1))


def join(s, ids, parts, grad, grad_send):
    return call(
        join_kernel,
        [shape(D, ROWS)] * 2,
        [whole(1, PAIR), whole(2, SENT, CHUNK), whole(D, ROWS), whole(D, ROWS)],
        [whole(D, ROWS)] * 2,
        [pltpu.VMEM((D, PAIR), F32)],
        4 * D * PAIR * 2 * ROWS,
        3 * 1024 * 1024,
    )(s, ids, parts, grad, grad_send)


def update_kernel(s_ref, grad_ref, got_ref, own_ref, state_ref, out_ref, out_state_ref):
    step_rows(grad_ref[...] + got_ref[...], own_ref, state_ref, out_ref, out_state_ref)


def update(s, grad, got, own, state):
    ins = [whole(D, ROWS)] * 2 + ROWS_SPECS
    return call(update_kernel, [shape(D, ROWS), shape(1, ROWS)], ins, ROWS_SPECS, [], 8 * D * ROWS, 16 * D * ROWS)(
        s, grad, got, own, state
    )


def count_in(s_ref, ids_ref, before_ref, out_ref, high_ref, low_ref):
    spots = hot(QUARTER, ids_ref[...], QUARTER * s_ref[0])
    total = dot2((high_ref[...], low_ref[...]), spots, (1, 1))
    for k in range(5):
        at = slice(D * k, D * k + D)
        tile = total[:, 128 * k : 128 * k + 128]
        out_ref[at, :] = tile if before_ref is None else before_ref[at, :] + tile
    out_ref[5 * D :, :] = jnp.zeros((KROWS - 5 * D, 128), F32)


def kinds_answered_kernel(s_ref, ids_ref, answers_ref, heads_ref, out_ref, high_ref, low_ref, d_ref, up_ref, a_ref):
    for k in range(4):
        unpack(a_ref, EVERY, heads_ref[k])
        unpack(up_ref, EVERY, answers_ref[k])
        back(d_ref, EVERY, up_ref[:HALF, :], up_ref[HALF:, :], a_ref[:HALF, :], a_ref[HALF:, :])
        high_ref[:, chunk_at(k)], low_ref[:, chunk_at(k)] = split(d_ref[...])
    count_in(s_ref, ids_ref, None, out_ref, high_ref, low_ref)


def kinds_kernel(s_ref, ids_ref, parts_ref, before_ref, out_ref, high_ref, low_ref, work_ref):
    for k in range(4):
        unpack(work_ref, EVERY, parts_ref[k])
        high_ref[:, chunk_at(k)], low_ref[:, chunk_at(k)] = split(work_ref[...])
    count_in(s_ref, ids_ref, before_ref, out_ref, high_ref, low_ref)


KINDS_COST = (4 * D * SLOTS * QUARTER, 3 * 1024 * 1024)


def kinds_answered(s, ids, answers, heads):
    ins = [whole(1, SLOTS)] + [whole(4, SENT, CHUNK)] * 2
    scratch = PARTS + [WORK] * 3
    return call(kinds_answered_kernel, shape(KROWS, 128), ins, whole(KROWS, 128), scratch, *KINDS_COST)(
        s, ids, answers, heads
    )


def kinds(s, ids, parts, before):
    ins = [whole(1, SLOTS), whole(4, SENT, CHUNK), whole(KROWS, 128)]
    return call(kinds_kernel, shape(KROWS, 128), ins, whole(KROWS, 128), PARTS + [WORK], *KINDS_COST)(s, ids, parts, before)


def relations_kernel(core_ref, grad_ref, table_ref, state_ref, *refs):
    out_ref, out_state_ref = refs[-2:]

    @pl.when(pl.program_id(0) == 0)
    def _():
        out_state_ref[...] = refs[1][...] if len(refs) > 2 else state_ref[...]

    for k in range(5):
        at = slice(128 * k, 128 * k + 128)
        row = pl.ds(5 * (2 * pl.program_id(0) + core_ref[0]) + k, 1)
        gradient = grad_ref[0, D * k : D * k + D, :]
        state = state_ref[row, :] + jnp.sum(gradient * gradient, axis=0, keepdims=True) * (1.0 / D)
        out_state_ref[row, :] = state
        out_ref[:, at] = table_ref[:, at] - gradient * (LEARN_RATE / (jnp.sqrt(state) + EPSILON))


def update_relations(core, grads, table, state, before):
    mine = pl.BlockSpec((D, QUARTER), lambda l, core: (0, 2 * l + core[0]))
    states = whole(RELATIONS // 128, 128)
    return call(
        relations_kernel,
        [shape(D, RELATIONS), shape(RELATIONS // 128, 128)],
        [pl.BlockSpec((1, KROWS, 128), lambda l, core: (l, 0, 0)), mine, states]
        + ([pl.BlockSpec(memory_space=pl.ANY), states] if before else []),
        [mine, states],
        [],
        5 * D * RELATIONS,
        6 * 1024 * 1024,
        grid=(2,),
        input_output_aliases={4: 0} if before else {},
    )(core, grads, table, state, *before)


def slot_lists(src_rows, rel_ids, dst_rows, live_count):
    live = jnp.arange(CAP, dtype=I32)[None, :] < live_count[0]
    lists = jnp.where(live[:, None, :], jnp.stack([src_rows[0], rel_ids[0], dst_rows[0]], axis=1), -1)
    every = lax.all_gather(lists.reshape(12, 128), REL, axis=0).reshape(4, 6, CAP)
    light = jnp.moveaxis(every[:, :, :LIGHT], 0, 1).reshape(6, 4 * LIGHT)
    heavy = jnp.max(every[:, :, LIGHT:], axis=0)
    chunks = jnp.concatenate([light, heavy], axis=1).reshape(6, 4, USED)
    return jnp.pad(chunks, ((0, 0), (0, 0), (0, CHUNK - USED)), constant_values=-1).reshape(6, SLOTS)


def local(entities, entity_state, relations, relation_state, src_rows, rel_ids, dst_rows, live_count, neg_rows):
    place = lax.axis_index(REL).astype(I32)
    core, chip, side = place & 1, place // 2, lax.axis_index("h").astype(I32)
    s = place.reshape(1)
    own, state = entities.T, entity_state.reshape(1, ROWS)
    table = relations.T
    pick = lambda lists, rows, at: lax.dynamic_slice_in_dim(lists.reshape(rows, -1), at, 1, 0)

    slots = slot_lists(src_rows, rel_ids, dst_rows, live_count)
    own, slots = tied((own, slots))
    other = flip(own, "l")
    near = lax.all_gather(own, "c", axis=0)
    chunk_ids, chunk_kinds, chunk_targets = [pick(slots[k], 4, place) for k in range(3)]
    chunk_rel = lookup(s, chunk_kinds[None], table)
    far = lax.all_gather(other, "c", axis=0)
    head, mail = letter(s, chunk_ids, near, far, chunk_rel, chunk_targets, neg_rows[0, 0].reshape(8, 128))
    mail, head, bucket_kinds = tied((mail, head, slots[1]))
    rel_rows = lookup(s, bucket_kinds.reshape(2, 1, PAIR), table)
    mail, head_rows, rel_rows = tied((flip(mail, "z", 8), lax.all_gather(head, REL, axis=0), rel_rows))
    keep, send, grad, grad_send = answer(s, lax.all_gather(mail, "c", axis=0), own, other)
    reply = keep + flip(send, "c")
    sent = jnp.concatenate([slots[4:6].reshape(8, 128), neg_rows[0, 1].reshape(8, 128)], axis=0)
    reply, sent = tied((reply, sent))
    got = flip(sent, "h")
    kind_ids, target_ids, negatives = got[:4].reshape(1, SLOTS), got[4:8], got[8:]
    later_rows = lookup(s, pick(kind_ids, 2, chip)[None], table)
    reply, grad_got, later_rows = tied((flip(reply, "z", 8), flip(grad_send, "l"), later_rows))
    answers = lax.all_gather(reply, REL, axis=0)
    own, state = update_answered(s, slots[0:1], answers, rel_rows, grad, grad_got, own, state)
    total = kinds_answered(s, slots[1:2], answers, head_rows)

    other = flip(own, "l")
    near = lax.all_gather(own, "c", axis=0)
    other, total = tied((other, total))
    chunk = heads(s, pick(slots[3], 4, place), near, lax.all_gather(other, "c", axis=0))
    head_rows = lax.all_gather(chunk, ("h", "c"), axis=0)
    beyond = jnp.stack([place, 2 * (1 - side)])
    keep, send, grad, grad_send, head, kind = score(beyond, pick(target_ids, 2, chip), negatives, head_rows, later_rows, own, other)
    d_head, d_kind = chunk_back(s, keep, flip(send, "c"), head, kind)
    d_kinds, d_head = tied((lax.all_gather(d_kind, REL, axis=0), flip(d_head, "h")))
    total = kinds(s, kind_ids, d_kinds, total)

    shares = lax.all_to_all(total.reshape(8, 256, 128), SPREAD, 0, 0)
    pieces = lax.all_to_all(jnp.sum(shares, axis=0).reshape(16, 16, 128), "z", 0, 0)
    grad, grad_send = join(s, pick(slots[3], 2, chip), lax.all_gather(d_head, "c", axis=0), grad, grad_send)
    pieces, grad, grad_send = tied((pieces, grad, grad_send))
    piece = jnp.sum(pieces, axis=0)
    share = lax.all_to_all(jnp.broadcast_to(piece[None], (16, 16, 128)), "z", 0, 0).reshape(256, 128)
    share, grad_got = tied((share, flip(grad_send, "l")))
    own, state = update(s, grad, grad_got, own, state)
    half = lax.all_to_all(jnp.broadcast_to(share[None], (16, 256, 128)), ("l",) + SPREAD, 0, 0).reshape(2, KROWS, 128)
    half, own, state = tied((half, own, state))
    table_state = relation_state.reshape(RELATIONS // 128, 128)
    first = update_relations(core.reshape(1), half, table, table_state, [])
    new_table, new_table_state = update_relations((1 - core).reshape(1), flip(half, "c"), table, table_state, first)
    return own.T, state.reshape(ROWS), new_table.T, new_table_state.reshape(RELATIONS)


def solution(mesh):
    fine = Mesh(mesh.devices.reshape(16, 4, 2, 2, 2), ("z", "y", "h", "l", "c"))
    dom, rel = ("z", "y", "h"), REL
    edge = P(dom, None, rel)
    in_specs = (P(dom + rel, None), P(dom + rel), P(), P(), edge, edge, edge, edge, P(dom, None, None))
    out_specs = (P(dom + rel, None), P(dom + rel), P(), P())
    return jax.shard_map(local, mesh=fine, in_specs=in_specs, out_specs=out_specs, check_vma=False)
```

```python
import functools

import jax
import jax.numpy as jnp
from jax import lax
from jax.experimental import pallas as pl
from jax.experimental.pallas import tpu as pltpu
from jax.sharding import Mesh, PartitionSpec as P

D = 400
HALF = 200
RELATIONS = 2560
NEG = 1024
CAP = 256
LIGHT = 64
SLOTS = 512
PAIR = 256
CHUNK = 128
USED = 112
SENT = 352
TAIL = D - SENT
ROWS = 256
QUARTER = RELATIONS // 4
PART = 512
KROWS = 2048
LETTER = SENT + 16
LEARN_RATE = 0.1
EPSILON = 1e-08
REL = ("l", "c")
SPREAD = ("y", "h")
F32, BF16, I32 = jnp.float32, jnp.bfloat16, jnp.int32
SMEM = pl.BlockSpec(memory_space=pltpu.SMEM)
tied = lax.optimization_barrier


def flip(block, axis, mask=1):
    count = lax.axis_size(axis)
    return lax.ppermute(block, axis, [(i, i ^ mask) for i in range(count)])


def split(value):
    high = value.astype(BF16)
    return high, (value - high.astype(F32)).astype(BF16)


def dot(first, second, over):
    return lax.dot_general(first, second, ((over[:1], over[1:]), ((), ())), preferred_element_type=F32)


def dot2(first, second, over):
    return dot(first[0], second, over) + dot(first[1], second, over)


def dot3(first, second, over):
    return dot(first[0], second[0], over) + (dot(first[0], second[1], over) + dot(first[1], second[0], over))


def places(rows, ids, base):
    return lax.broadcasted_iota(I32, (rows, ids.shape[-1]), 0) + base == ids


def hot(rows, ids, base):
    return jnp.where(places(rows, ids, base), 1.0, 0.0).astype(BF16)


def times(out_ref, at, a1, a2, w1, w2):
    out_ref[:HALF, at] = a1 * w1 - a2 * w2
    out_ref[HALF:D, at] = a1 * w2 + a2 * w1


def back(out_ref, at, u1, u2, o1, o2):
    out_ref[:HALF, at] = u1 * o1 + u2 * o2
    out_ref[HALF:D, at] = u2 * o1 - u1 * o2


def pack(out_ref, value):
    lanes = lax.broadcasted_iota(I32, (TAIL, CHUNK), 1)
    out_ref[:SENT, :] = value[:SENT, :]
    for group in range(USED // 16):
        at = slice(TAIL * group, TAIL * group + TAIL)
        moved = pltpu.roll(value[SENT:, :], (USED - 16 * group) % CHUNK, 1)
        out_ref[at, :] = jnp.where(lanes >= USED, moved, value[at, :])


def unpack(out_ref, at, value):
    lanes = lax.broadcasted_iota(I32, (TAIL, CHUNK), 1)
    out_ref[:SENT, at] = value
    rest = jnp.zeros((TAIL, CHUNK), F32)
    for group in range(USED // 16):
        moved = pltpu.roll(value[TAIL * group : TAIL * group + TAIL, :], (16 * group - USED) % CHUNK, 1)
        rest = jnp.where(lanes // 16 == group, moved, rest)
    out_ref[SENT:, at] = rest


EVERY = slice(None)
WORK = pltpu.VMEM((D, CHUNK), F32)


def shape(*dims):
    return jax.ShapeDtypeStruct(dims, F32)


def whole(*dims):
    return pl.BlockSpec(dims, lambda *_: (0,) * len(dims))


def call(kernel, out_shape, in_specs, out_specs, scratch, flops, moved, grid=(1,), room=40, **more):
    return pl.pallas_call(
        kernel,
        out_shape=out_shape,
        grid_spec=pltpu.PrefetchScalarGridSpec(
            num_scalar_prefetch=1, grid=grid, in_specs=in_specs, out_specs=out_specs, scratch_shapes=scratch
        ),
        compiler_params=pltpu.CompilerParams(vmem_limit_bytes=room * 1024 * 1024),
        cost_estimate=pl.CostEstimate(flops=flops, bytes_accessed=moved, transcendentals=0),
        **more,
    )


def lookup_kernel(s_ref, ids_ref, table_ref, out_ref):
    step = pl.program_id(0)
    table = split(table_ref[...])
    for k in range(ids_ref.shape[0]):
        found = dot2(table, hot(PART, ids_ref[k], PART * step), (1, 0))

        @pl.when(step == 0)
        def _():
            out_ref[k] = found

        @pl.when(step > 0)
        def _():
            out_ref[k] += found


def lookup(s, ids, table):
    lists, _, width = ids.shape
    return call(
        lookup_kernel,
        shape(lists, D, width),
        [whole(lists, 1, width), pl.BlockSpec((D, PART), lambda i, s: (0, i))],
        whole(lists, D, width),
        [],
        4 * D * RELATIONS * lists * width,
        5 * 1024 * 1024,
        grid=(RELATIONS // PART,),
        room=56,
    )(s, ids, table)


def chunk_rows(q, ids, near_ref, far_ref):
    first = q & 2
    total = jnp.zeros((D, CHUNK), F32)
    for ref, base in ((near_ref, first), (far_ref, first ^ 2)):
        for k in range(2):
            total += dot2(split(ref[k]), hot(ROWS, ids, ROWS * (base + k)), (1, 0))
    return total


def heads_kernel(s_ref, ids_ref, near_ref, far_ref, out_ref):
    pack(out_ref, chunk_rows(s_ref[0], ids_ref[...], near_ref, far_ref))


def halves_kernel(s_ref, ids_ref, near_ref, mine_ref, theirs_ref):
    first = s_ref[0] & 2
    rows = [split(near_ref[k]) for k in range(2)]
    for which, out_ref in enumerate((mine_ref, theirs_ref)):
        ids = ids_ref[which : which + 1, :]
        pack(out_ref, sum(dot2(rows[k], hot(ROWS, ids, ROWS * (first + k)), (1, 0)) for k in range(2)))


def letter_kernel(s_ref, mine_ref, got_ref, rel_ref, target_ref, neg_ref, head_ref, out_ref, work_ref, a_ref):
    head_ref[...] = mine_ref[...] + got_ref[...]
    unpack(a_ref, EVERY, head_ref[...])
    times(work_ref, EVERY, a_ref[:HALF, :], a_ref[HALF:, :], rel_ref[0, :HALF, :], rel_ref[0, HALF:, :])
    pack(out_ref, work_ref[...])
    out_ref[SENT : SENT + 8, :] = jnp.broadcast_to(target_ref[...], (8, CHUNK)).astype(F32)
    out_ref[SENT + 8 :, :] = neg_ref[...].astype(F32)


HEADS_IN = [whole(1, CHUNK), whole(2, D, ROWS), whole(2, D, ROWS)]
HEADS_COST = (4 * D * 1024 * CHUNK, 2 * 1024 * 1024)


def heads(s, ids, near, far):
    return call(heads_kernel, shape(SENT, CHUNK), HEADS_IN, whole(SENT, CHUNK), [], *HEADS_COST)(s, ids, near, far)


def halves(s, ids, near):
    sent = whole(SENT, CHUNK)
    return call(halves_kernel, [shape(SENT, CHUNK)] * 2, [whole(2, CHUNK), whole(2, D, ROWS)], [sent] * 2, [], *HEADS_COST)(
        s, ids, near
    )


def letter(s, mine, got, rel_rows, target, negatives):
    sent = whole(SENT, CHUNK)
    return call(
        letter_kernel,
        [shape(SENT, CHUNK), shape(LETTER, CHUNK)],
        [sent, sent, whole(1, D, CHUNK), whole(1, CHUNK), whole(8, 128)],
        [sent, whole(LETTER, CHUNK)],
        [WORK] * 2,
        10 * D * CHUNK,
        20 * D * CHUNK,
    )(s, mine, got, rel_rows, target, negatives)


def weigh(s_ref, h_ref, target, negatives, own_ref, other_ref, keep_ref, send_ref, grad_ref, grad_send_ref):
    q = s_ref[0]
    product = split(h_ref[...])
    live = jnp.where(target >= 0, 1.0 / NEG, 0.0)
    d_product = jnp.zeros((D, PAIR), F32)
    for k, (ref, out_ref) in enumerate(((own_ref, grad_ref), (other_ref, grad_send_ref))):
        base = ROWS * (q ^ (2 * k))
        hits = jnp.zeros((ROWS, 128), F32)
        for row in range(8):
            hits += jnp.where(places(ROWS, negatives[row : row + 1, :], base), 1.0, 0.0)
        rows = split(ref[...])
        scores = dot3(rows, product, (0, 0))
        small = jnp.exp(-jnp.abs(scores))
        larger = 1.0 / (1.0 + small)
        smaller = small * larger
        rising = scores >= 0
        weight = jnp.where(rising, larger, smaller) * jnp.sum(hits, axis=1, keepdims=True) * live
        weight -= jnp.where(places(ROWS, target, base), jnp.where(rising, smaller, larger), 0.0)
        weight = split(weight)
        d_product += dot3(rows, weight, (1, 0))
        out_ref[...] = dot3(product, weight, (1, 1))
    h_ref[...] = d_product
    core = q & 1
    pack(keep_ref, h_ref[:, pl.ds(pl.multiple_of(CHUNK * core, CHUNK), CHUNK)])
    pack(send_ref, h_ref[:, pl.ds(pl.multiple_of(CHUNK * (1 - core), CHUNK), CHUNK)])


def answer_kernel(s_ref, letters_ref, own_ref, other_ref, keep_ref, send_ref, grad_ref, grad_send_ref, h_ref):
    for k in range(2):
        unpack(h_ref, slice(CHUNK * k, CHUNK * k + CHUNK), letters_ref[k, :SENT, :])
    target = jnp.concatenate([letters_ref[k, SENT : SENT + 1, :] for k in range(2)], axis=1).astype(I32)
    negatives = letters_ref[0, SENT + 8 :, :].astype(I32)
    weigh(s_ref, h_ref, target, negatives, own_ref, other_ref, keep_ref, send_ref, grad_ref, grad_send_ref)


def answer(s, letters, own, other):
    return call(
        answer_kernel,
        [shape(SENT, CHUNK)] * 2 + [shape(D, ROWS)] * 2,
        [whole(2, LETTER, CHUNK), whole(D, ROWS), whole(D, ROWS)],
        [whole(SENT, CHUNK)] * 2 + [whole(D, ROWS)] * 2,
        [pltpu.VMEM((D, PAIR), F32)],
        1024 * 1024 * 1024,
        5 * 1024 * 1024,
    )(s, letters, own, other)


def score_kernel(s_ref, target_ref, neg_ref, a_ref, rel_ref, own_ref, other_ref, keep_ref, send_ref, grad_ref, grad_send_ref, head_ref, kind_ref, h_ref, work_ref):
    first = s_ref[1]
    for k in range(2):
        at = slice(CHUNK * k, CHUNK * k + CHUNK)
        unpack(work_ref, at, a_ref[first + k])
        times(h_ref, at, work_ref[:HALF, at], work_ref[HALF:, at], rel_ref[0, :HALF, at], rel_ref[0, HALF:, at])
    weigh(s_ref, h_ref, target_ref[...], neg_ref[...], own_ref, other_ref, keep_ref, send_ref, grad_ref, grad_send_ref)
    core = s_ref[0] & 1
    mine = pl.ds(pl.multiple_of(CHUNK * core, CHUNK), CHUNK)
    head_ref[...] = work_ref[:, mine]
    kind_ref[...] = rel_ref[0, :, mine]


def score(s, target, negatives, head_rows, rel_rows, own, other):
    return call(
        score_kernel,
        [shape(SENT, CHUNK)] * 2 + [shape(D, ROWS)] * 2 + [shape(D, CHUNK)] * 2,
        [
            whole(1, PAIR),
            whole(8, 128),
            whole(4, SENT, CHUNK),
            whole(1, D, PAIR),
            whole(D, ROWS),
            whole(D, ROWS),
        ],
        [whole(SENT, CHUNK)] * 2 + [whole(D, ROWS)] * 2 + [whole(D, CHUNK)] * 2,
        [pltpu.VMEM((D, PAIR), F32)] * 2,
        1024 * 1024 * 1024,
        5 * 1024 * 1024,
    )(s, target, negatives, head_rows, rel_rows, own, other)


def back_kernel(s_ref, keep_ref, got_ref, head_ref, kind_ref, d_head_ref, d_kind_ref, up_ref, work_ref):
    unpack(up_ref, EVERY, keep_ref[...] + got_ref[...])
    for other_ref, out_ref in ((kind_ref, d_head_ref), (head_ref, d_kind_ref)):
        back(work_ref, EVERY, up_ref[:HALF, :], up_ref[HALF:, :], other_ref[:HALF, :], other_ref[HALF:, :])
        pack(out_ref, work_ref[...])


def chunk_back(s, keep, got, head, kind):
    sent, chunk = whole(SENT, CHUNK), whole(D, CHUNK)
    out = [shape(SENT, CHUNK)] * 2
    ins = [sent] * 2 + [chunk] * 2
    return call(back_kernel, out, ins, [sent] * 2, [WORK] * 2, 10 * D * CHUNK, 32 * D * CHUNK)(s, keep, got, head, kind)


def step_rows(gradient, own_ref, state_ref, out_ref, out_state_ref):
    state = state_ref[...] + jnp.sum(gradient * gradient, axis=0, keepdims=True) * (1.0 / D)
    out_state_ref[...] = state
    out_ref[...] = own_ref[...] - gradient * (LEARN_RATE / (jnp.sqrt(state) + EPSILON))


def chunk_at(k):
    return slice(CHUNK * k, CHUNK * k + CHUNK)


def answered_kernel(s_ref, ids_ref, answers_ref, rel_ref, grad_ref, got_ref, own_ref, state_ref, out_ref, out_state_ref, high_ref, low_ref, d_ref, up_ref):
    for k in range(4):
        at = chunk_at(k % 2)
        w1, w2 = rel_ref[k // 2, :HALF, at], rel_ref[k // 2, HALF:, at]
        unpack(up_ref, EVERY, answers_ref[k])
        back(d_ref, EVERY, up_ref[:HALF, :], up_ref[HALF:, :], w1, w2)
        high_ref[:, chunk_at(k)], low_ref[:, chunk_at(k)] = split(d_ref[...])
    spots = hot(ROWS, ids_ref[...], ROWS * s_ref[0])
    gradient = grad_ref[...] + got_ref[...] + dot2((high_ref[...], low_ref[...]), spots, (1, 1))
    step_rows(gradient, own_ref, state_ref, out_ref, out_state_ref)


ROWS_SPECS = [whole(D, ROWS), whole(1, ROWS)]
PARTS = [pltpu.VMEM((D, SLOTS), BF16)] * 2


def update_answered(s, ids, answers, rel_rows, grad, got, own, state):
    return call(
        answered_kernel,
        [shape(D, ROWS), shape(1, ROWS)],
        [whole(1, SLOTS), whole(4, SENT, CHUNK), whole(2, D, PAIR), whole(D, ROWS), whole(D, ROWS)] + ROWS_SPECS,
        ROWS_SPECS,
        PARTS + [WORK] * 2,
        4 * D * SLOTS * ROWS,
        4 * 1024 * 1024,
    )(s, ids, answers, rel_rows, grad, got, own, state)


def join_kernel(s_ref, ids_ref, parts_ref, grad_ref, send_ref, out_ref, out_send_ref, work_ref):
    for k in range(2):
        unpack(work_ref, chunk_at(k), parts_ref[k])
    parts = split(work_ref[...])
    for flipped, ref, to_ref in ((0, grad_ref, out_ref), (2, send_ref, out_send_ref)):
        base = ROWS * (s_ref[0] ^ flipped)
        to_ref[...] = ref[...] + dot2(parts, hot(ROWS, ids_ref[...], base), (1, 1))


def join(s, ids, parts, grad, grad_send):
    return call(
        join_kernel,
        [shape(D, ROWS)] * 2,
        [whole(1, PAIR), whole(2, SENT, CHUNK), whole(D, ROWS), whole(D, ROWS)],
        [whole(D, ROWS)] * 2,
        [pltpu.VMEM((D, PAIR), F32)],
        4 * D * PAIR * 2 * ROWS,
        3 * 1024 * 1024,
    )(s, ids, parts, grad, grad_send)


def update_kernel(s_ref, grad_ref, got_ref, own_ref, state_ref, out_ref, out_state_ref):
    step_rows(grad_ref[...] + got_ref[...], own_ref, state_ref, out_ref, out_state_ref)


def update(s, grad, got, own, state):
    ins = [whole(D, ROWS)] * 2 + ROWS_SPECS
    return call(update_kernel, [shape(D, ROWS), shape(1, ROWS)], ins, ROWS_SPECS, [], 8 * D * ROWS, 16 * D * ROWS)(
        s, grad, got, own, state
    )


def count_in(s_ref, ids_ref, before_ref, out_ref, high_ref, low_ref):
    spots = hot(QUARTER, ids_ref[...], QUARTER * s_ref[0])
    total = dot2((high_ref[...], low_ref[...]), spots, (1, 1))
    for k in range(5):
        at = slice(D * k, D * k + D)
        tile = total[:, 128 * k : 128 * k + 128]
        out_ref[at, :] = tile if before_ref is None else before_ref[at, :] + tile
    out_ref[5 * D :, :] = jnp.zeros((KROWS - 5 * D, 128), F32)


def kinds_answered_kernel(s_ref, ids_ref, answers_ref, heads_ref, out_ref, high_ref, low_ref, d_ref, up_ref, a_ref):
    for k in range(4):
        unpack(a_ref, EVERY, heads_ref[k])
        unpack(up_ref, EVERY, answers_ref[k])
        back(d_ref, EVERY, up_ref[:HALF, :], up_ref[HALF:, :], a_ref[:HALF, :], a_ref[HALF:, :])
        high_ref[:, chunk_at(k)], low_ref[:, chunk_at(k)] = split(d_ref[...])
    count_in(s_ref, ids_ref, None, out_ref, high_ref, low_ref)


def kinds_kernel(s_ref, ids_ref, parts_ref, before_ref, out_ref, high_ref, low_ref, work_ref):
    for k in range(4):
        unpack(work_ref, EVERY, parts_ref[k])
        high_ref[:, chunk_at(k)], low_ref[:, chunk_at(k)] = split(work_ref[...])
    count_in(s_ref, ids_ref, before_ref, out_ref, high_ref, low_ref)


KINDS_COST = (4 * D * SLOTS * QUARTER, 3 * 1024 * 1024)


def kinds_answered(s, ids, answers, heads):
    ins = [whole(1, SLOTS)] + [whole(4, SENT, CHUNK)] * 2
    scratch = PARTS + [WORK] * 3
    return call(kinds_answered_kernel, shape(KROWS, 128), ins, whole(KROWS, 128), scratch, *KINDS_COST)(
        s, ids, answers, heads
    )


def kinds(s, ids, parts, before):
    ins = [whole(1, SLOTS), whole(4, SENT, CHUNK), whole(KROWS, 128)]
    return call(kinds_kernel, shape(KROWS, 128), ins, whole(KROWS, 128), PARTS + [WORK], *KINDS_COST)(s, ids, parts, before)


def relations_kernel(core_ref, grad_ref, table_ref, state_ref, *refs):
    out_ref, out_state_ref = refs[-2:]

    @pl.when(pl.program_id(0) == 0)
    def _():
        out_state_ref[...] = refs[1][...] if len(refs) > 2 else state_ref[...]

    for k in range(5):
        at = slice(128 * k, 128 * k + 128)
        row = pl.ds(5 * (2 * pl.program_id(0) + core_ref[0]) + k, 1)
        gradient = grad_ref[0, D * k : D * k + D, :]
        state = state_ref[row, :] + jnp.sum(gradient * gradient, axis=0, keepdims=True) * (1.0 / D)
        out_state_ref[row, :] = state
        out_ref[:, at] = table_ref[:, at] - gradient * (LEARN_RATE / (jnp.sqrt(state) + EPSILON))


def update_relations(core, grads, table, state, before):
    mine = pl.BlockSpec((D, QUARTER), lambda l, core: (0, 2 * l + core[0]))
    states = whole(RELATIONS // 128, 128)
    return call(
        relations_kernel,
        [shape(D, RELATIONS), shape(RELATIONS // 128, 128)],
        [pl.BlockSpec((1, KROWS, 128), lambda l, core: (l, 0, 0)), mine, states]
        + ([pl.BlockSpec(memory_space=pl.ANY), states] if before else []),
        [mine, states],
        [],
        5 * D * RELATIONS,
        6 * 1024 * 1024,
        grid=(2,),
        input_output_aliases={4: 0} if before else {},
    )(core, grads, table, state, *before)


def slot_lists(src_rows, rel_ids, dst_rows, live_count):
    live = jnp.arange(CAP, dtype=I32)[None, :] < live_count[0]
    lists = jnp.where(live[:, None, :], jnp.stack([src_rows[0], rel_ids[0], dst_rows[0]], axis=1), -1)
    every = lax.all_gather(lists.reshape(12, 128), REL, axis=0).reshape(4, 6, CAP)
    light = jnp.moveaxis(every[:, :, :LIGHT], 0, 1).reshape(6, 4 * LIGHT)
    heavy = jnp.max(every[:, :, LIGHT:], axis=0)
    chunks = jnp.concatenate([light, heavy], axis=1).reshape(6, 4, USED)
    return jnp.pad(chunks, ((0, 0), (0, 0), (0, CHUNK - USED)), constant_values=-1).reshape(6, SLOTS)


def local(entities, entity_state, relations, relation_state, src_rows, rel_ids, dst_rows, live_count, neg_rows):
    place = lax.axis_index(REL).astype(I32)
    core, chip, side = place & 1, place // 2, lax.axis_index("h").astype(I32)
    s = place.reshape(1)
    own, state = entities.T, entity_state.reshape(1, ROWS)
    table = relations.T
    pick = lambda lists, rows, at: lax.dynamic_slice_in_dim(lists.reshape(rows, -1), at, 1, 0)

    near = lax.all_gather(own, "c", axis=0)
    slots = slot_lists(src_rows, rel_ids, dst_rows, live_count)
    chunk_ids, chunk_kinds, chunk_targets = [pick(slots[k], 4, place) for k in range(3)]
    mine, theirs = halves(s, jnp.concatenate([chunk_ids, pick(slots[0], 4, place ^ 2)]), near)
    chunk_rel = lookup(s, chunk_kinds[None], table)
    head, mail = letter(s, mine, flip(theirs, "l"), chunk_rel, chunk_targets, neg_rows[0, 0].reshape(8, 128))
    mail, head, own, bucket_kinds = tied((mail, head, own, slots[1]))
    other = flip(own, "l")
    rel_rows = lookup(s, bucket_kinds.reshape(2, 1, PAIR), table)
    mail, other, rel_rows = tied((flip(mail, "z", 8), other, rel_rows))
    keep, send, grad, grad_send = answer(s, lax.all_gather(mail, "c", axis=0), own, other)
    reply = keep + flip(send, "c")
    reply, head = tied((reply, head))
    head_rows = lax.all_gather(head, REL, axis=0)
    sent = jnp.concatenate([slots[4:6].reshape(8, 128), neg_rows[0, 1].reshape(8, 128)], axis=0)
    head_rows, sent = tied((head_rows, sent))
    reply, grad_got, got = tied((flip(reply, "z", 8), flip(grad_send, "l"), flip(sent, "h")))
    kind_ids, target_ids, negatives = got[:4].reshape(1, SLOTS), got[4:8], got[8:]
    answers = lax.all_gather(reply, REL, axis=0)
    own, state = update_answered(s, slots[0:1], answers, rel_rows, grad, grad_got, own, state)
    total = kinds_answered(s, slots[1:2], answers, head_rows)

    other = flip(own, "l")
    near = lax.all_gather(own, "c", axis=0)
    later_rows = lookup(s, pick(kind_ids, 2, chip)[None], table)
    other, total, later_rows = tied((other, total, later_rows))
    chunk = heads(s, pick(slots[3], 4, place), near, lax.all_gather(other, "c", axis=0))
    head_rows = lax.all_gather(chunk, ("h", "c"), axis=0)
    beyond = jnp.stack([place, 2 * (1 - side)])
    keep, send, grad, grad_send, head, kind = score(beyond, pick(target_ids, 2, chip), negatives, head_rows, later_rows, own, other)
    d_head, d_kind = chunk_back(s, keep, flip(send, "c"), head, kind)
    total = kinds(s, kind_ids, lax.all_gather(d_kind, REL, axis=0), total)

    total, d_head = tied((total, d_head))
    shares, d_head = tied((lax.all_to_all(total.reshape(8, 256, 128), SPREAD, 0, 0), flip(d_head, "h")))
    pieces = lax.all_to_all(jnp.sum(shares, axis=0).reshape(16, 16, 128), "z", 0, 0)
    grad, grad_send = join(s, pick(slots[3], 2, chip), lax.all_gather(d_head, "c", axis=0), grad, grad_send)
    pieces, grad, grad_send = tied((pieces, grad, grad_send))
    piece = jnp.sum(pieces, axis=0)
    share = lax.all_to_all(jnp.broadcast_to(piece[None], (16, 16, 128)), "z", 0, 0).reshape(256, 128)
    share, grad_got = tied((share, flip(grad_send, "l")))
    own, state = update(s, grad, grad_got, own, state)
    half = lax.all_to_all(jnp.broadcast_to(share[None], (16, 256, 128)), ("l",) + SPREAD, 0, 0).reshape(2, KROWS, 128)
    half, own, state = tied((half, own, state))
    table_state = relation_state.reshape(RELATIONS // 128, 128)
    first = update_relations(core.reshape(1), half, table, table_state, [])
    new_table, new_table_state = update_relations((1 - core).reshape(1), flip(half, "c"), table, table_state, first)
    return own.T, state.reshape(ROWS), new_table.T, new_table_state.reshape(RELATIONS)


def solution(mesh):
    fine = Mesh(mesh.devices.reshape(16, 4, 2, 2, 2), ("z", "y", "h", "l", "c"))
    dom, rel = ("z", "y", "h"), REL
    edge = P(dom, None, rel)
    in_specs = (P(dom + rel, None), P(dom + rel), P(), P(), edge, edge, edge, edge, P(dom, None, None))
    out_specs = (P(dom + rel, None), P(dom + rel), P(), P())
    return jax.shard_map(local, mesh=fine, in_specs=in_specs, out_specs=out_specs, check_vma=False)
```

```python
import functools

import jax
import jax.numpy as jnp
from jax import lax
from jax.experimental import pallas as pl
from jax.experimental.pallas import tpu as pltpu
from jax.sharding import Mesh, PartitionSpec as P

D = 400
HALF = 200
RELATIONS = 2560
NEG = 1024
CAP = 256
LIGHT = 64
SLOTS = 512
PAIR = 256
CHUNK = 128
USED = 112
SENT = 352
TAIL = D - SENT
ROWS = 256
QUARTER = RELATIONS // 4
PART = 512
KROWS = 2048
LETTER = SENT + 16
LEARN_RATE = 0.1
EPSILON = 1e-08
REL = ("l", "c")
SPREAD = ("y", "h")
F32, BF16, I32 = jnp.float32, jnp.bfloat16, jnp.int32
SMEM = pl.BlockSpec(memory_space=pltpu.SMEM)
tied = lax.optimization_barrier


def flip(block, axis, mask=1):
    count = lax.axis_size(axis)
    return lax.ppermute(block, axis, [(i, i ^ mask) for i in range(count)])


def split(value):
    high = value.astype(BF16)
    return high, (value - high.astype(F32)).astype(BF16)


def dot(first, second, over):
    return lax.dot_general(first, second, ((over[:1], over[1:]), ((), ())), preferred_element_type=F32)


def dot2(first, second, over):
    return dot(first[0], second, over) + dot(first[1], second, over)


def dot3(first, second, over):
    return dot(first[0], second[0], over) + (dot(first[0], second[1], over) + dot(first[1], second[0], over))


def places(rows, ids, base):
    return lax.broadcasted_iota(I32, (rows, ids.shape[-1]), 0) + base == ids


def hot(rows, ids, base):
    return jnp.where(places(rows, ids, base), 1.0, 0.0).astype(BF16)


def times(out_ref, at, a1, a2, w1, w2):
    out_ref[:HALF, at] = a1 * w1 - a2 * w2
    out_ref[HALF:D, at] = a1 * w2 + a2 * w1


def back(out_ref, at, u1, u2, o1, o2):
    out_ref[:HALF, at] = u1 * o1 + u2 * o2
    out_ref[HALF:D, at] = u2 * o1 - u1 * o2


def pack(out_ref, value):
    lanes = lax.broadcasted_iota(I32, (TAIL, CHUNK), 1)
    out_ref[:SENT, :] = value[:SENT, :]
    for group in range(USED // 16):
        at = slice(TAIL * group, TAIL * group + TAIL)
        moved = pltpu.roll(value[SENT:, :], (USED - 16 * group) % CHUNK, 1)
        out_ref[at, :] = jnp.where(lanes >= USED, moved, value[at, :])


def unpack(out_ref, at, value):
    lanes = lax.broadcasted_iota(I32, (TAIL, CHUNK), 1)
    out_ref[:SENT, at] = value
    rest = jnp.zeros((TAIL, CHUNK), F32)
    for group in range(USED // 16):
        moved = pltpu.roll(value[TAIL * group : TAIL * group + TAIL, :], (16 * group - USED) % CHUNK, 1)
        rest = jnp.where(lanes // 16 == group, moved, rest)
    out_ref[SENT:, at] = rest


EVERY = slice(None)
WORK = pltpu.VMEM((D, CHUNK), F32)


def shape(*dims):
    return jax.ShapeDtypeStruct(dims, F32)


def whole(*dims):
    return pl.BlockSpec(dims, lambda *_: (0,) * len(dims))


def call(kernel, out_shape, in_specs, out_specs, scratch, flops, moved, grid=(1,), room=40, **more):
    return pl.pallas_call(
        kernel,
        out_shape=out_shape,
        grid_spec=pltpu.PrefetchScalarGridSpec(
            num_scalar_prefetch=1, grid=grid, in_specs=in_specs, out_specs=out_specs, scratch_shapes=scratch
        ),
        compiler_params=pltpu.CompilerParams(vmem_limit_bytes=room * 1024 * 1024),
        cost_estimate=pl.CostEstimate(flops=flops, bytes_accessed=moved, transcendentals=0),
        **more,
    )


def lookup_kernel(s_ref, ids_ref, table_ref, out_ref):
    step = pl.program_id(0)
    table = split(table_ref[...])
    for k in range(ids_ref.shape[0]):
        found = dot2(table, hot(PART, ids_ref[k], PART * step), (1, 0))

        @pl.when(step == 0)
        def _():
            out_ref[k] = found

        @pl.when(step > 0)
        def _():
            out_ref[k] += found


def lookup(s, ids, table, room=56):
    lists, _, width = ids.shape
    return call(
        lookup_kernel,
        shape(lists, D, width),
        [whole(lists, 1, width), pl.BlockSpec((D, PART), lambda i, s: (0, i))],
        whole(lists, D, width),
        [],
        4 * D * RELATIONS * lists * width,
        5 * 1024 * 1024,
        grid=(RELATIONS // PART,),
        room=room,
    )(s, ids, table)


def chunk_rows(q, ids, near_ref, far_ref):
    first = q & 2
    total = jnp.zeros((D, CHUNK), F32)
    for ref, base in ((near_ref, first), (far_ref, first ^ 2)):
        for k in range(2):
            total += dot2(split(ref[k]), hot(ROWS, ids, ROWS * (base + k)), (1, 0))
    return total


def heads_kernel(s_ref, ids_ref, near_ref, far_ref, out_ref):
    pack(out_ref, chunk_rows(s_ref[0], ids_ref[...], near_ref, far_ref))


def halves_kernel(s_ref, ids_ref, near_ref, mine_ref, theirs_ref):
    first = s_ref[0] & 2
    rows = [split(near_ref[k]) for k in range(2)]
    for which, out_ref in enumerate((mine_ref, theirs_ref)):
        ids = ids_ref[which : which + 1, :]
        pack(out_ref, sum(dot2(rows[k], hot(ROWS, ids, ROWS * (first + k)), (1, 0)) for k in range(2)))


def letter_kernel(s_ref, mine_ref, got_ref, rel_ref, target_ref, neg_ref, head_ref, out_ref, work_ref, a_ref):
    head_ref[...] = mine_ref[...] + got_ref[...]
    unpack(a_ref, EVERY, head_ref[...])
    times(work_ref, EVERY, a_ref[:HALF, :], a_ref[HALF:, :], rel_ref[0, :HALF, :], rel_ref[0, HALF:, :])
    pack(out_ref, work_ref[...])
    out_ref[SENT : SENT + 8, :] = jnp.broadcast_to(target_ref[...], (8, CHUNK)).astype(F32)
    out_ref[SENT + 8 :, :] = neg_ref[...].astype(F32)


HEADS_IN = [whole(1, CHUNK), whole(2, D, ROWS), whole(2, D, ROWS)]
HEADS_COST = (4 * D * 1024 * CHUNK, 2 * 1024 * 1024)


def heads(s, ids, near, far):
    return call(heads_kernel, shape(SENT, CHUNK), HEADS_IN, whole(SENT, CHUNK), [], *HEADS_COST)(s, ids, near, far)


def halves(s, ids, near):
    sent = whole(SENT, CHUNK)
    return call(halves_kernel, [shape(SENT, CHUNK)] * 2, [whole(2, CHUNK), whole(2, D, ROWS)], [sent] * 2, [], *HEADS_COST)(
        s, ids, near
    )


def letter(s, mine, got, rel_rows, target, negatives):
    sent = whole(SENT, CHUNK)
    return call(
        letter_kernel,
        [shape(SENT, CHUNK), shape(LETTER, CHUNK)],
        [sent, sent, whole(1, D, CHUNK), whole(1, CHUNK), whole(8, 128)],
        [sent, whole(LETTER, CHUNK)],
        [WORK] * 2,
        10 * D * CHUNK,
        20 * D * CHUNK,
    )(s, mine, got, rel_rows, target, negatives)


def weigh(s_ref, h_ref, target, negatives, own_ref, other_ref, keep_ref, send_ref, grad_ref, grad_send_ref):
    q = s_ref[0]
    product = split(h_ref[...])
    live = jnp.where(target >= 0, 1.0 / NEG, 0.0)
    d_product = jnp.zeros((D, PAIR), F32)
    for k, (ref, out_ref) in enumerate(((own_ref, grad_ref), (other_ref, grad_send_ref))):
        base = ROWS * (q ^ (2 * k))
        hits = jnp.zeros((ROWS, 128), F32)
        for row in range(8):
            hits += jnp.where(places(ROWS, negatives[row : row + 1, :], base), 1.0, 0.0)
        rows = split(ref[...])
        scores = dot3(rows, product, (0, 0))
        small = jnp.exp(-jnp.abs(scores))
        larger = 1.0 / (1.0 + small)
        smaller = small * larger
        rising = scores >= 0
        weight = jnp.where(rising, larger, smaller) * jnp.sum(hits, axis=1, keepdims=True) * live
        weight -= jnp.where(places(ROWS, target, base), jnp.where(rising, smaller, larger), 0.0)
        weight = split(weight)
        d_product += dot3(rows, weight, (1, 0))
        out_ref[...] = dot3(product, weight, (1, 1))
    h_ref[...] = d_product
    core = q & 1
    pack(keep_ref, h_ref[:, pl.ds(pl.multiple_of(CHUNK * core, CHUNK), CHUNK)])
    pack(send_ref, h_ref[:, pl.ds(pl.multiple_of(CHUNK * (1 - core), CHUNK), CHUNK)])


def answer_kernel(s_ref, letters_ref, own_ref, other_ref, keep_ref, send_ref, grad_ref, grad_send_ref, h_ref):
    for k in range(2):
        unpack(h_ref, slice(CHUNK * k, CHUNK * k + CHUNK), letters_ref[k, :SENT, :])
    target = jnp.concatenate([letters_ref[k, SENT : SENT + 1, :] for k in range(2)], axis=1).astype(I32)
    negatives = letters_ref[0, SENT + 8 :, :].astype(I32)
    weigh(s_ref, h_ref, target, negatives, own_ref, other_ref, keep_ref, send_ref, grad_ref, grad_send_ref)


def answer(s, letters, own, other):
    return call(
        answer_kernel,
        [shape(SENT, CHUNK)] * 2 + [shape(D, ROWS)] * 2,
        [whole(2, LETTER, CHUNK), whole(D, ROWS), whole(D, ROWS)],
        [whole(SENT, CHUNK)] * 2 + [whole(D, ROWS)] * 2,
        [pltpu.VMEM((D, PAIR), F32)],
        1024 * 1024 * 1024,
        5 * 1024 * 1024,
    )(s, letters, own, other)


def score_kernel(s_ref, target_ref, neg_ref, a_ref, rel_ref, own_ref, other_ref, keep_ref, send_ref, grad_ref, grad_send_ref, head_ref, kind_ref, h_ref, work_ref):
    first = s_ref[1]
    for k in range(2):
        at = slice(CHUNK * k, CHUNK * k + CHUNK)
        unpack(work_ref, at, a_ref[first + k])
        times(h_ref, at, work_ref[:HALF, at], work_ref[HALF:, at], rel_ref[0, :HALF, at], rel_ref[0, HALF:, at])
    weigh(s_ref, h_ref, target_ref[...], neg_ref[...], own_ref, other_ref, keep_ref, send_ref, grad_ref, grad_send_ref)
    core = s_ref[0] & 1
    mine = pl.ds(pl.multiple_of(CHUNK * core, CHUNK), CHUNK)
    head_ref[...] = work_ref[:, mine]
    kind_ref[...] = rel_ref[0, :, mine]


def score(s, target, negatives, head_rows, rel_rows, own, other):
    return call(
        score_kernel,
        [shape(SENT, CHUNK)] * 2 + [shape(D, ROWS)] * 2 + [shape(D, CHUNK)] * 2,
        [
            whole(1, PAIR),
            whole(8, 128),
            whole(4, SENT, CHUNK),
            whole(1, D, PAIR),
            whole(D, ROWS),
            whole(D, ROWS),
        ],
        [whole(SENT, CHUNK)] * 2 + [whole(D, ROWS)] * 2 + [whole(D, CHUNK)] * 2,
        [pltpu.VMEM((D, PAIR), F32)] * 2,
        1024 * 1024 * 1024,
        5 * 1024 * 1024,
    )(s, target, negatives, head_rows, rel_rows, own, other)


def back_kernel(s_ref, keep_ref, got_ref, head_ref, kind_ref, d_head_ref, d_kind_ref, up_ref, work_ref):
    unpack(up_ref, EVERY, keep_ref[...] + got_ref[...])
    for other_ref, out_ref in ((kind_ref, d_head_ref), (head_ref, d_kind_ref)):
        back(work_ref, EVERY, up_ref[:HALF, :], up_ref[HALF:, :], other_ref[:HALF, :], other_ref[HALF:, :])
        pack(out_ref, work_ref[...])


def chunk_back(s, keep, got, head, kind):
    sent, chunk = whole(SENT, CHUNK), whole(D, CHUNK)
    out = [shape(SENT, CHUNK)] * 2
    ins = [sent] * 2 + [chunk] * 2
    return call(back_kernel, out, ins, [sent] * 2, [WORK] * 2, 10 * D * CHUNK, 32 * D * CHUNK)(s, keep, got, head, kind)


def step_rows(gradient, own_ref, state_ref, out_ref, out_state_ref):
    state = state_ref[...] + jnp.sum(gradient * gradient, axis=0, keepdims=True) * (1.0 / D)
    out_state_ref[...] = state
    out_ref[...] = own_ref[...] - gradient * (LEARN_RATE / (jnp.sqrt(state) + EPSILON))


def chunk_at(k):
    return slice(CHUNK * k, CHUNK * k + CHUNK)


def answered_kernel(s_ref, ids_ref, answers_ref, rel_ref, grad_ref, got_ref, own_ref, state_ref, out_ref, out_state_ref, high_ref, low_ref, d_ref, up_ref):
    for k in range(4):
        at = chunk_at(k % 2)
        w1, w2 = rel_ref[k // 2, :HALF, at], rel_ref[k // 2, HALF:, at]
        unpack(up_ref, EVERY, answers_ref[k])
        back(d_ref, EVERY, up_ref[:HALF, :], up_ref[HALF:, :], w1, w2)
        high_ref[:, chunk_at(k)], low_ref[:, chunk_at(k)] = split(d_ref[...])
    spots = hot(ROWS, ids_ref[...], ROWS * s_ref[0])
    gradient = grad_ref[...] + got_ref[...] + dot2((high_ref[...], low_ref[...]), spots, (1, 1))
    step_rows(gradient, own_ref, state_ref, out_ref, out_state_ref)


ROWS_SPECS = [whole(D, ROWS), whole(1, ROWS)]
PARTS = [pltpu.VMEM((D, SLOTS), BF16)] * 2


def update_answered(s, ids, answers, rel_rows, grad, got, own, state):
    return call(
        answered_kernel,
        [shape(D, ROWS), shape(1, ROWS)],
        [whole(1, SLOTS), whole(4, SENT, CHUNK), whole(2, D, PAIR), whole(D, ROWS), whole(D, ROWS)] + ROWS_SPECS,
        ROWS_SPECS,
        PARTS + [WORK] * 2,
        4 * D * SLOTS * ROWS,
        4 * 1024 * 1024,
    )(s, ids, answers, rel_rows, grad, got, own, state)


def join_kernel(s_ref, ids_ref, parts_ref, grad_ref, send_ref, out_ref, out_send_ref, work_ref):
    for k in range(2):
        unpack(work_ref, chunk_at(k), parts_ref[k])
    parts = split(work_ref[...])
    for flipped, ref, to_ref in ((0, grad_ref, out_ref), (2, send_ref, out_send_ref)):
        base = ROWS * (s_ref[0] ^ flipped)
        to_ref[...] = ref[...] + dot2(parts, hot(ROWS, ids_ref[...], base), (1, 1))


def join(s, ids, parts, grad, grad_send):
    return call(
        join_kernel,
        [shape(D, ROWS)] * 2,
        [whole(1, PAIR), whole(2, SENT, CHUNK), whole(D, ROWS), whole(D, ROWS)],
        [whole(D, ROWS)] * 2,
        [pltpu.VMEM((D, PAIR), F32)],
        4 * D * PAIR * 2 * ROWS,
        3 * 1024 * 1024,
    )(s, ids, parts, grad, grad_send)


def update_kernel(s_ref, grad_ref, got_ref, own_ref, state_ref, out_ref, out_state_ref):
    step_rows(grad_ref[...] + got_ref[...], own_ref, state_ref, out_ref, out_state_ref)


def update(s, grad, got, own, state):
    ins = [whole(D, ROWS)] * 2 + ROWS_SPECS
    return call(update_kernel, [shape(D, ROWS), shape(1, ROWS)], ins, ROWS_SPECS, [], 8 * D * ROWS, 16 * D * ROWS)(
        s, grad, got, own, state
    )


def count_in(s_ref, ids_ref, before_ref, out_ref, high_ref, low_ref):
    spots = hot(QUARTER, ids_ref[...], QUARTER * s_ref[0])
    total = dot2((high_ref[...], low_ref[...]), spots, (1, 1))
    for k in range(5):
        at = slice(D * k, D * k + D)
        tile = total[:, 128 * k : 128 * k + 128]
        out_ref[at, :] = tile if before_ref is None else before_ref[at, :] + tile
    out_ref[5 * D :, :] = jnp.zeros((KROWS - 5 * D, 128), F32)


def kinds_answered_kernel(s_ref, ids_ref, answers_ref, heads_ref, out_ref, high_ref, low_ref, d_ref, up_ref, a_ref):
    for k in range(4):
        unpack(a_ref, EVERY, heads_ref[k])
        unpack(up_ref, EVERY, answers_ref[k])
        back(d_ref, EVERY, up_ref[:HALF, :], up_ref[HALF:, :], a_ref[:HALF, :], a_ref[HALF:, :])
        high_ref[:, chunk_at(k)], low_ref[:, chunk_at(k)] = split(d_ref[...])
    count_in(s_ref, ids_ref, None, out_ref, high_ref, low_ref)


def kinds_kernel(s_ref, ids_ref, parts_ref, before_ref, out_ref, high_ref, low_ref, work_ref):
    for k in range(4):
        unpack(work_ref, EVERY, parts_ref[k])
        high_ref[:, chunk_at(k)], low_ref[:, chunk_at(k)] = split(work_ref[...])
    count_in(s_ref, ids_ref, before_ref, out_ref, high_ref, low_ref)


KINDS_COST = (4 * D * SLOTS * QUARTER, 3 * 1024 * 1024)


def kinds_answered(s, ids, answers, heads):
    ins = [whole(1, SLOTS)] + [whole(4, SENT, CHUNK)] * 2
    scratch = PARTS + [WORK] * 3
    return call(kinds_answered_kernel, shape(KROWS, 128), ins, whole(KROWS, 128), scratch, *KINDS_COST)(
        s, ids, answers, heads
    )


def kinds(s, ids, parts, before):
    ins = [whole(1, SLOTS), whole(4, SENT, CHUNK), whole(KROWS, 128)]
    return call(kinds_kernel, shape(KROWS, 128), ins, whole(KROWS, 128), PARTS + [WORK], *KINDS_COST)(s, ids, parts, before)


def relations_kernel(core_ref, grad_ref, table_ref, state_ref, *refs):
    out_ref, out_state_ref = refs[-2:]

    @pl.when(pl.program_id(0) == 0)
    def _():
        out_state_ref[...] = refs[1][...] if len(refs) > 2 else state_ref[...]

    for k in range(5):
        at = slice(128 * k, 128 * k + 128)
        row = pl.ds(5 * (2 * pl.program_id(0) + core_ref[0]) + k, 1)
        gradient = grad_ref[0, D * k : D * k + D, :]
        state = state_ref[row, :] + jnp.sum(gradient * gradient, axis=0, keepdims=True) * (1.0 / D)
        out_state_ref[row, :] = state
        out_ref[:, at] = table_ref[:, at] - gradient * (LEARN_RATE / (jnp.sqrt(state) + EPSILON))


def update_relations(core, grads, table, state, before):
    mine = pl.BlockSpec((D, QUARTER), lambda l, core: (0, 2 * l + core[0]))
    states = whole(RELATIONS // 128, 128)
    return call(
        relations_kernel,
        [shape(D, RELATIONS), shape(RELATIONS // 128, 128)],
        [pl.BlockSpec((1, KROWS, 128), lambda l, core: (l, 0, 0)), mine, states]
        + ([pl.BlockSpec(memory_space=pl.ANY), states] if before else []),
        [mine, states],
        [],
        5 * D * RELATIONS,
        6 * 1024 * 1024,
        grid=(2,),
        input_output_aliases={4: 0} if before else {},
    )(core, grads, table, state, *before)


def slot_lists(src_rows, rel_ids, dst_rows, live_count):
    live = jnp.arange(CAP, dtype=I32)[None, :] < live_count[0]
    lists = jnp.where(live[:, None, :], jnp.stack([src_rows[0], rel_ids[0], dst_rows[0]], axis=1), -1)
    every = lax.all_gather(lists.reshape(12, 128), REL, axis=0).reshape(4, 6, CAP)
    light = jnp.moveaxis(every[:, :, :LIGHT], 0, 1).reshape(6, 4 * LIGHT)
    heavy = jnp.max(every[:, :, LIGHT:], axis=0)
    chunks = jnp.concatenate([light, heavy], axis=1).reshape(6, 4, USED)
    return jnp.pad(chunks, ((0, 0), (0, 0), (0, CHUNK - USED)), constant_values=-1).reshape(6, SLOTS)


def local(entities, entity_state, relations, relation_state, src_rows, rel_ids, dst_rows, live_count, neg_rows):
    place = lax.axis_index(REL).astype(I32)
    core, chip, side = place & 1, place // 2, lax.axis_index("h").astype(I32)
    s = place.reshape(1)
    own, state = entities.T, entity_state.reshape(1, ROWS)
    table = relations.T
    pick = lambda lists, rows, at: lax.dynamic_slice_in_dim(lists.reshape(rows, -1), at, 1, 0)

    near = lax.all_gather(own, "c", axis=0)
    slots = slot_lists(src_rows, rel_ids, dst_rows, live_count)
    chunk_ids, chunk_kinds, chunk_targets = [pick(slots[k], 4, place) for k in range(3)]
    mine, theirs = halves(s, jnp.concatenate([chunk_ids, pick(slots[0], 4, place ^ 2)]), near)
    chunk_rel = lookup(s, chunk_kinds[None], table, room=40)
    head, mail = letter(s, mine, flip(theirs, "l"), chunk_rel, chunk_targets, neg_rows[0, 0].reshape(8, 128))
    mail, head, own, bucket_kinds = tied((mail, head, own, slots[1]))
    other = flip(own, "l")
    rel_rows = lookup(s, bucket_kinds.reshape(2, 1, PAIR), table)
    mail, other, rel_rows = tied((flip(mail, "z", 8), other, rel_rows))
    keep, send, grad, grad_send = answer(s, lax.all_gather(mail, "c", axis=0), own, other)
    reply = keep + flip(send, "c")
    reply, head = tied((reply, head))
    head_rows = lax.all_gather(head, REL, axis=0)
    sent = jnp.concatenate([slots[4:6].reshape(8, 128), neg_rows[0, 1].reshape(8, 128)], axis=0)
    head_rows, sent = tied((head_rows, sent))
    reply, grad_got, got = tied((flip(reply, "z", 8), flip(grad_send, "l"), flip(sent, "h")))
    kind_ids, target_ids, negatives = got[:4].reshape(1, SLOTS), got[4:8], got[8:]
    answers = lax.all_gather(reply, REL, axis=0)
    own, state = update_answered(s, slots[0:1], answers, rel_rows, grad, grad_got, own, state)
    total = kinds_answered(s, slots[1:2], answers, head_rows)

    other = flip(own, "l")
    near = lax.all_gather(own, "c", axis=0)
    later_rows = lookup(s, pick(kind_ids, 2, chip)[None], table)
    other, total, later_rows = tied((other, total, later_rows))
    chunk = heads(s, pick(slots[3], 4, place), near, lax.all_gather(other, "c", axis=0))
    head_rows = lax.all_gather(chunk, ("h", "c"), axis=0)
    beyond = jnp.stack([place, 2 * (1 - side)])
    keep, send, grad, grad_send, head, kind = score(beyond, pick(target_ids, 2, chip), negatives, head_rows, later_rows, own, other)
    d_head, d_kind = chunk_back(s, keep, flip(send, "c"), head, kind)
    total = kinds(s, kind_ids, lax.all_gather(d_kind, REL, axis=0), total)

    total, d_head = tied((total, d_head))
    shares, d_head = tied((lax.all_to_all(total.reshape(8, 256, 128), SPREAD, 0, 0), flip(d_head, "h")))
    pieces = lax.all_to_all(jnp.sum(shares, axis=0).reshape(16, 16, 128), "z", 0, 0)
    grad, grad_send = join(s, pick(slots[3], 2, chip), lax.all_gather(d_head, "c", axis=0), grad, grad_send)
    pieces, grad, grad_send = tied((pieces, grad, grad_send))
    piece = jnp.sum(pieces, axis=0)
    share = lax.all_to_all(jnp.broadcast_to(piece[None], (16, 16, 128)), "z", 0, 0).reshape(256, 128)
    share, grad_got = tied((share, flip(grad_send, "l")))
    own, state = update(s, grad, grad_got, own, state)
    half = lax.all_to_all(jnp.broadcast_to(share[None], (16, 256, 128)), ("l",) + SPREAD, 0, 0).reshape(2, KROWS, 128)
    half, own, state = tied((half, own, state))
    table_state = relation_state.reshape(RELATIONS // 128, 128)
    first = update_relations(core.reshape(1), half, table, table_state, [])
    new_table, new_table_state = update_relations((1 - core).reshape(1), flip(half, "c"), table, table_state, first)
    return own.T, state.reshape(ROWS), new_table.T, new_table_state.reshape(RELATIONS)


def solution(mesh):
    fine = Mesh(mesh.devices.reshape(16, 4, 2, 2, 2), ("z", "y", "h", "l", "c"))
    dom, rel = ("z", "y", "h"), REL
    edge = P(dom, None, rel)
    in_specs = (P(dom + rel, None), P(dom + rel), P(), P(), edge, edge, edge, edge, P(dom, None, None))
    out_specs = (P(dom + rel, None), P(dom + rel), P(), P())
    return jax.shard_map(local, mesh=fine, in_specs=in_specs, out_specs=out_specs, check_vma=False)
```
